32 devices in a mesh: cuts: 4 (over z), energy: 2 (over y), group: 4 (over x, core).
Axes of the slice: x: 2, y: 2, z: 4, core: 2. Of those that a mesh axis runs over, the one named last changes fastest.
Arguments:
- transfer: float32 [2, 12, 512, 512], P('energy', 'cuts'), may hold values from -1.5 to 1.5
- source: float32 [2, 6144, 512], P('energy', 'cuts', 'group'), may hold values from -4 to 4
- coupling: bfloat16 [512, 512], replicated, may hold values from -0.25 to 0.25
- strength: float32 [8], replicated, may hold values from 0.2 to 1
- mode_shift: int32 [8], replicated, may hold values from 0 to 1, as said below
Outputs:
- green: float32 [2, 6144, 512], P('energy', 'cuts', 'group')
- scattered: float32 [2, 6144, 512], P('energy', 'cuts', 'group')
The draws below stay inside these ranges and needn't reach their ends.
Inputs may be any that keep to these rules, and one draw needn't show every extreme that they name: `mode_shift`: every energy offset of 0 to 1 is taken by at least one mode.
All inputs are finite; a program needn't handle non-finite values.
Results may differ from the reference program's by a relative error of at most 0.0035.
Values sent between devices are 32-bit elements; how exact they have to be, the bound alone decides.
No kernel may reach another device: no remote copies, remote signals or barrier semaphores. Data moves between devices by JAX's collectives and lax.ppermute only.
A program may use at most 64 MiB of HBM per device.

```python
import math
import jax
import jax.numpy as jnp
from jax import lax

ORB = 512
MODES = 8
ENERGIES = 2
CHAIN_BLOCKS = 12
COLUMNS = 512


def draw_transfer(key, part):
    random_keys = jax.random.split(key, 7)
    slow_share = 0.5
    slow = jax.random.bernoulli(random_keys[0], slow_share, (ENERGIES, 1, ORB))
    slow_rate = jax.random.uniform(random_keys[1], (ENERGIES, 1, ORB), jnp.float32, 0.2, 0.8) / CHAIN_BLOCKS
    fast_rate = jax.random.uniform(random_keys[2], (ENERGIES, 1, ORB), jnp.float32, 0.5, 1.2)
    rate = jnp.where(slow, slow_rate, fast_rate)
    spread = jnp.exp(jax.random.uniform(random_keys[3], (ENERGIES, CHAIN_BLOCKS, ORB), jnp.float32, -0.35, 0.35))
    spike_location = jax.random.randint(random_keys[4], (2,), 0, CHAIN_BLOCKS)
    spike_event = jnp.any(jnp.arange(CHAIN_BLOCKS)[:, None] == spike_location[None, :], axis=1)
    decay_loss = jax.random.uniform(random_keys[5], (ENERGIES, CHAIN_BLOCKS, ORB), jnp.float32, 0.2, 0.4)
    retained_flags = jnp.where(spike_event[None, :, None], 1.0 - decay_loss, 1.0)
    diagonal = jnp.exp(-rate * spread) * retained_flags
    noise = jnp.clip(jax.random.normal(random_keys[6], (ENERGIES, CHAIN_BLOCKS, ORB, ORB), jnp.float32), -4.0, 4.0)
    noise = noise * (0.15 / jnp.sqrt(jnp.float32(ORB)))
    return noise + jnp.eye(ORB, dtype=jnp.float32) * diagonal[..., None, :]


def draw_mode_shift(key, part):
    shift_keys = jax.random.split(jax.random.fold_in(key, 71), 3)
    covered = jax.random.permutation(shift_keys[0], ENERGIES).astype(jnp.int32)
    extra = jax.random.randint(shift_keys[1], (MODES - ENERGIES,), 0, ENERGIES).astype(jnp.int32)
    joined = jnp.concatenate([covered, extra])
    order = jax.random.permutation(shift_keys[2], MODES)
    return joined[order].astype(jnp.int32)


def levels(rng, shape, shards, low, top_value):
    def one(position, parts):
        heights = jax.random.uniform(jax.random.fold_in(jax.random.fold_in(rng, 6), position), (parts,), jnp.float32, low / len(shards), top_value / len(shards))
        return jnp.repeat(jnp.exp(heights), shape[position] // parts).reshape((-1,) + (1,) * (len(shape) - position - 1))

    gain = one(*shards[0])
    for cut in shards[1:]:
        gain = gain * one(*cut)
    return gain


def scatter_about(stream_key, extent, scale, bound, pieces=(), kind=jnp.bfloat16):
    level = levels(stream_key, extent, pieces, -0.22, 0.18) if pieces else 1.0
    values = jax.random.normal(stream_key, extent, jnp.float32) * scale * level
    return jnp.minimum(jnp.maximum(values, -bound), bound).astype(kind)


def setup_inputs(seed: int = 0) -> dict:
    key_list = jax.random.split(jax.random.key(seed), 6)
    transfer = draw_transfer(jax.random.fold_in(key_list[5], 71), 0)
    source = scatter_about(key_list[1], (ENERGIES, CHAIN_BLOCKS * ORB, COLUMNS), 0.5, 4.0, ((0, 2), (1, 4), (2, 4)), jnp.float32)
    coupling = scatter_about(key_list[2], (ORB, ORB), ORB ** -0.5, 0.25)
    strength = jnp.clip(jnp.exp(jax.random.uniform(key_list[3], (MODES,), jnp.float32, math.log(0.2), math.log(1.0))), 0.2, 1.0)
    mode_shift = draw_mode_shift(jax.random.fold_in(key_list[5], 71), 0)
    return dict(transfer=transfer, source=source, coupling=coupling, strength=strength, mode_shift=mode_shift)


def propagate(mats, srcs):
    def advance(carry, item):
        matrix, piece = item
        fresh = jnp.dot(matrix, carry, precision=lax.Precision.HIGHEST, preferred_element_type=jnp.float32) + piece
        return fresh, fresh

    start = jnp.zeros((ORB, COLUMNS), jnp.float32)
    _, chain_states = lax.scan(advance, start, (mats, srcs))
    return chain_states


def reference(transfer, source, coupling, strength, mode_shift):
    blocks_src = source.reshape(ENERGIES, CHAIN_BLOCKS, ORB, COLUMNS)
    green = lax.map(lambda pair: propagate(pair[0], pair[1]), (transfer, blocks_src))
    density = jnp.mean(green * green, axis=3)
    padded = jnp.pad(density, ((0, 0), (1, 1), (0, 0)))
    smoothed = density + 0.5 * (padded[:, :-2] + padded[:, 2:])
    goal_value = (jnp.arange(ENERGIES, dtype=jnp.int32)[:, None] + mode_shift[None, :]) % ENERGIES
    onehot = (goal_value[:, :, None] == jnp.arange(ENERGIES, dtype=jnp.int32)[None, None, :]).astype(jnp.float32)
    mixing = jnp.sum(strength[None, :, None] * onehot, axis=1)
    selfen = jnp.einsum("ef,fko->eko", mixing, smoothed, precision=lax.Precision.HIGHEST)
    low = green.astype(jnp.bfloat16).astype(jnp.float32)
    wide = coupling.astype(jnp.float32)
    inner = jnp.einsum("oi,ekon->ekin", wide, low)
    scaled = (inner * selfen[..., None]).astype(jnp.bfloat16).astype(jnp.float32)
    scattered = jnp.einsum("io,ekon->ekin", wide, scaled)
    return green.reshape(ENERGIES, CHAIN_BLOCKS * ORB, COLUMNS), scattered.reshape(ENERGIES, CHAIN_BLOCKS * ORB, COLUMNS)
```

```python
import functools

import jax
import jax.numpy as jnp
from jax import lax
from jax.experimental import pallas as pl
from jax.experimental.pallas import tpu as pltpu
from jax.sharding import PartitionSpec as P

F32 = jnp.float32
BF16 = jnp.bfloat16
VMEM = pl.BlockSpec(memory_space=pltpu.VMEM)
HBM = pl.BlockSpec(memory_space=pltpu.HBM)
PARAMS = pltpu.CompilerParams(vmem_limit_bytes=48 * 1024 * 1024)


def split(value):
    high = value.astype(BF16)
    return high, (value - high.astype(F32)).astype(BF16)


def dot(left, right):
    return jnp.dot(left, right, preferred_element_type=F32)


def dot_t(left, right):
    return lax.dot_general(left, right, (((1,), (1,)), ((), ())), preferred_element_type=F32)


def product(left_high, left_low, state):
    high, low = split(state)
    width = state.shape[1]
    both = dot(left_high, jnp.concatenate([high, low], axis=1))
    return both[:, :width] + (both[:, width:] + dot(left_low, high))


def local_kernel(mats_ref, srcs_ref, local_ref, mats, srcs, sems, src_sem):
    count, orbs = mats_ref.shape[0], mats_ref.shape[1]
    src_copy = pltpu.make_async_copy(srcs_ref, srcs, src_sem)
    src_copy.start()
    copies = [
        pltpu.make_async_copy(mats_ref.at[k], mats.at[k], sems.at[k]) for k in range(1, count)
    ]
    for copy in copies:
        copy.start()
    src_copy.wait()
    state = srcs[:orbs, :]
    local_ref[:orbs, :] = state
    for k in range(1, count):
        copies[k - 1].wait()
        rows = slice(k * orbs, (k + 1) * orbs)
        state = product(*split(mats[k]), state) + srcs[rows, :]
        local_ref[rows, :] = state


def local_chain(mats, srcs):
    return pl.pallas_call(
        local_kernel,
        out_shape=jax.ShapeDtypeStruct(srcs.shape, F32),
        in_specs=[HBM, HBM],
        out_specs=VMEM,
        scratch_shapes=[
            pltpu.VMEM(mats.shape, F32),
            pltpu.VMEM(srcs.shape, F32),
            pltpu.SemaphoreType.DMA((mats.shape[0],)),
            pltpu.SemaphoreType.DMA,
        ],
        compiler_params=PARAMS,
        name="local_chain",
    )(mats, srcs)


def composite_kernel(mats_ref, high_ref, low_ref, mats, sems):
    count, orbs = mats_ref.shape[0], mats_ref.shape[1]
    copies = [pltpu.make_async_copy(mats_ref.at[k], mats.at[k], sems.at[k]) for k in range(count)]
    for copy in copies:
        copy.start()
    copies[0].wait()
    high, low = split(mats[0])
    high_ref[:orbs, :], low_ref[:orbs, :] = high, low
    for k in range(1, count):
        copies[k].wait()
        left_high, left_low = split(mats[k])
        full = dot(left_high, high) + (dot(left_high, low) + dot(left_low, high))
        high, low = split(full)
        rows = slice(k * orbs, (k + 1) * orbs)
        high_ref[rows, :], low_ref[rows, :] = high, low


def composites(mats):
    count, orbs, _ = mats.shape
    shape = jax.ShapeDtypeStruct((count * orbs, orbs), BF16)
    return pl.pallas_call(
        composite_kernel,
        out_shape=(shape, shape),
        in_specs=[HBM],
        out_specs=(VMEM, VMEM),
        scratch_shapes=[pltpu.VMEM(mats.shape, F32), pltpu.SemaphoreType.DMA((count,))],
        compiler_params=PARAMS,
        cost_estimate=pl.CostEstimate(
            flops=6 * (count - 1) * orbs**3, bytes_accessed=8 * count * orbs**2, transcendentals=0
        ),
        name="composites",
    )(mats)


def relay_kernel(step, high_ref, low_ref, local_ref, got_ref, incoming_ref, out_ref, kept_ref):
    orbs = got_ref.shape[0]
    got = got_ref[...]
    rows = slice(high_ref.shape[0] - orbs, None)
    out_ref[...] = product(high_ref[rows, :], low_ref[rows, :], got) + local_ref[rows, :]
    kept_ref[...] = jnp.where(lax.axis_index("cuts") == step, got, incoming_ref[...])


def relay(step, high, low, local, got, incoming):
    shape = jax.ShapeDtypeStruct(got.shape, F32)
    return pl.pallas_call(
        functools.partial(relay_kernel, step),
        out_shape=(shape, shape),
        in_specs=[VMEM] * 5,
        out_specs=(VMEM, VMEM),
        compiler_params=PARAMS,
        name="relay",
    )(high, low, local, got, incoming)


def row_sums(value):
    squares = value * value
    high, low = split(squares)
    ones = jnp.ones((8, value.shape[1]), BF16)
    return (dot_t(ones, high) + dot_t(ones, low))[:1, :]


def green_kernel(step, high_ref, low_ref, local_ref, got_ref, incoming_ref, green_ref, sums_ref):
    orbs = got_ref.shape[0]
    count = local_ref.shape[0] // orbs
    state = jnp.where(lax.axis_index("cuts") == step, got_ref[...], incoming_ref[...])
    sums = [row_sums(state)]
    for k in range(count):
        rows = slice(k * orbs, (k + 1) * orbs)
        block = product(high_ref[rows, :], low_ref[rows, :], state) + local_ref[rows, :]
        green_ref[rows, :] = block
        sums.append(row_sums(block))
    sums_ref[...] = jnp.concatenate(sums, axis=0)


def green_blocks(step, high, low, local, got, incoming):
    orbs = got.shape[0]
    count = local.shape[0] // orbs
    return pl.pallas_call(
        functools.partial(green_kernel, step),
        out_shape=(
            jax.ShapeDtypeStruct(local.shape, F32),
            jax.ShapeDtypeStruct((count + 1, orbs), F32),
        ),
        in_specs=[VMEM] * 5,
        out_specs=(VMEM, VMEM),
        compiler_params=PARAMS,
        name="green_blocks",
    )(high, low, local, got, incoming)


def inner_kernel(coupling_ref, green_ref, inner_ref):
    orbs = coupling_ref.shape[0]
    coupling = coupling_ref[...]
    for k in range(green_ref.shape[0] // orbs):
        low = green_ref[k * orbs : (k + 1) * orbs, :].astype(BF16)
        inner_ref[k] = dot(low.T, coupling)


def inner_blocks(coupling, green):
    orbs = coupling.shape[0]
    count, width = green.shape[0] // orbs, green.shape[1]
    return pl.pallas_call(
        inner_kernel,
        out_shape=jax.ShapeDtypeStruct((count, width, orbs), F32),
        in_specs=[VMEM, VMEM],
        out_specs=VMEM,
        compiler_params=PARAMS,
        cost_estimate=pl.CostEstimate(
            flops=2 * count * width * orbs**2, bytes_accessed=2 * orbs**2, transcendentals=0
        ),
        name="inner_blocks",
    )(coupling, green)


def scatter_kernel(coupling_ref, inner_ref, mixed_ref, after_ref, out_ref):
    count, _, orbs = inner_ref.shape
    rows = [mixed_ref[k : k + 1, :] for k in range(count + 1)]
    last = lax.axis_index("cuts") == lax.axis_size("cuts") - 1
    rows.append(jnp.where(last, 0.0, after_ref[...]))
    coupling = coupling_ref[...]
    for k in range(count):
        selfen = rows[k + 1] + 0.5 * (rows[k] + rows[k + 2])
        scaled = (inner_ref[k] * selfen).astype(BF16)
        out_ref[k * orbs : (k + 1) * orbs, :] = dot_t(coupling, scaled)


def scatter_blocks(coupling, inner, mixed, after):
    count, width, orbs = inner.shape
    return pl.pallas_call(
        scatter_kernel,
        out_shape=jax.ShapeDtypeStruct((count * orbs, width), F32),
        in_specs=[VMEM] * 4,
        out_specs=VMEM,
        compiler_params=PARAMS,
        name="scatter_blocks",
    )(coupling, inner, mixed, after)


def relay_pairs(step, cuts, group):
    pairs = []
    for c in range(cuts):
        for g in range(group):
            if c == step - 1:
                to = (c + 1, g)
            elif c == step:
                to = (c - 1, g)
            else:
                to = (c, g ^ 1 if g ^ 1 < group else g)
            pairs.append((c * group + g, to[0] * group + to[1]))
    return pairs


def exchanged(value, axis, offset):
    devices = lax.axis_size(axis)
    return lax.ppermute(value, axis, [(i, (i + offset) % devices) for i in range(devices)])


def body(transfer, source, coupling, strength, mode_shift):
    mats, srcs = transfer[0], source[0]
    orbs, width = mats.shape[1], srcs.shape[1]
    cuts, group, points = (lax.axis_size(a) for a in ("cuts", "group", "energy"))
    local = local_chain(mats, srcs)
    leaving = local[local.shape[0] - orbs :, :]
    incoming = jnp.zeros((orbs, width), F32)
    high, low = composites(mats)
    got = incoming
    for step in range(1, cuts):
        got = lax.ppermute(leaving, ("cuts", "group"), relay_pairs(step, cuts, group))
        if step < cuts - 1:
            leaving, incoming = relay(step, high, low, local, got, incoming)
    green, sums = green_blocks(cuts - 1, high, low, local, got, incoming)
    inner = inner_blocks(coupling, green)

    parts = [exchanged(sums, "group", offset) for offset in range(1, group)]
    density = (sums + sum(parts)) / (width * group)
    here = lax.axis_index("energy")
    goal = (here + mode_shift) % points
    mixed = 0.0
    for offset in range(points):
        there = density if offset == 0 else exchanged(density, "energy", offset)
        weight = jnp.sum(jnp.where(goal == (here - offset) % points, strength, 0.0))
        mixed = mixed + weight * there
    after = exchanged(mixed[1:2], "cuts", -1)
    scattered = scatter_blocks(coupling, inner, mixed, after)
    return green[None], scattered[None]


def solution(mesh):
    in_specs = (P("energy", "cuts", None, None), P("energy", "cuts", "group"), P(), P(), P())
    out_specs = (P("energy", "cuts", "group"), P("energy", "cuts", "group"))
    return jax.shard_map(body, mesh=mesh, in_specs=in_specs, out_specs=out_specs, check_vma=False)
```

```python
import functools

import jax
import jax.numpy as jnp
from jax import lax
from jax.experimental import pallas as pl
from jax.experimental.pallas import tpu as pltpu
from jax.sharding import PartitionSpec as P

F32 = jnp.float32
BF16 = jnp.bfloat16
VMEM = pl.BlockSpec(memory_space=pltpu.VMEM)
SMEM = pl.BlockSpec(memory_space=pltpu.SMEM)
HBM = pl.BlockSpec(memory_space=pltpu.HBM)
PARAMS = pltpu.CompilerParams(vmem_limit_bytes=32 * 1024 * 1024)
WHOLE = pltpu.CompilerParams(vmem_limit_bytes=53 * 1024 * 1024)
PIECES = 2


def split(value):
    high = value.astype(BF16)
    return high, (value - high.astype(F32)).astype(BF16)


def dot(left, right):
    return jnp.dot(left, right, preferred_element_type=F32)


def dot_t(left, right):
    return lax.dot_general(left, right, (((1,), (1,)), ((), ())), preferred_element_type=F32)


def product(left_high, left_low, state):
    high, low = split(state)
    width = state.shape[1]
    both = dot(left_high, jnp.concatenate([high, low], axis=1))
    return both[:, :width] + (both[:, width:] + dot(left_low, high))


def product_rows(state, right_high, right_low):
    high, low = split(state)
    height = state.shape[0]
    both = dot(jnp.concatenate([high, low], axis=0), right_high)
    return both[:height] + (both[height:] + dot(high, right_low))


def local_kernel(mats_ref, srcs_ref, *rest):
    outs, (mats, srcs, sems, src_sem) = rest[:-4], rest[-4:]
    middle_ref, leaving_refs = outs[0], outs[1:]
    count, orbs = mats_ref.shape[0], mats_ref.shape[1]
    src_copy = pltpu.make_async_copy(srcs_ref, srcs, src_sem)
    copies = [
        pltpu.make_async_copy(mats_ref.at[k], mats.at[k], sems.at[k]) for k in range(1, count)
    ]
    src_copy.start()
    for copy in copies:
        copy.start()
    src_copy.wait()
    state = srcs[:orbs, :]
    for k in range(1, count):
        copies[k - 1].wait()
        state = product(*split(mats[k]), state) + srcs[k * orbs : (k + 1) * orbs, :]
        if k < count - 1:
            middle_ref[k - 1] = state
    turned = state.T
    height = turned.shape[0] // len(leaving_refs)
    for piece, leaving_ref in enumerate(leaving_refs):
        leaving_ref[...] = turned[piece * height : (piece + 1) * height, :]


def local_chain(mats, srcs, pieces):
    count, orbs, _ = mats.shape
    width = srcs.shape[1]
    leaving = jax.ShapeDtypeStruct((width // pieces, orbs), F32)
    outs = pl.pallas_call(
        local_kernel,
        out_shape=(jax.ShapeDtypeStruct((count - 2, orbs, width), F32),) + (leaving,) * pieces,
        in_specs=[HBM, HBM],
        out_specs=(VMEM,) * (1 + pieces),
        scratch_shapes=[
            pltpu.VMEM(mats.shape, F32),
            pltpu.VMEM(srcs.shape, F32),
            pltpu.SemaphoreType.DMA((count,)),
            pltpu.SemaphoreType.DMA,
        ],
        compiler_params=WHOLE,
        name="local_chain",
    )(mats, srcs)
    return outs[0], list(outs[1:])


def composite_kernel(mats_ref, middle_ref, high_ref, low_ref):
    full = mats_ref[0]
    count = mats_ref.shape[0]
    for k in range(1, count):
        left_high, left_low = split(mats_ref[k])
        high, low = split(full)
        full = dot(left_high, high) + (dot(left_high, low) + dot(left_low, high))
        if k < count - 1:
            middle_ref[k - 1] = full
    high_ref[...], low_ref[...] = split(full.T)


def composites(mats):
    count, orbs, _ = mats.shape
    shape = jax.ShapeDtypeStruct((orbs, orbs), BF16)
    return pl.pallas_call(
        composite_kernel,
        out_shape=(jax.ShapeDtypeStruct((count - 2, orbs, orbs), F32), shape, shape),
        in_specs=[VMEM],
        out_specs=(VMEM,) * 3,
        compiler_params=PARAMS,
        cost_estimate=pl.CostEstimate(
            flops=6 * (count - 1) * orbs**3, bytes_accessed=8 * count * orbs**2, transcendentals=0
        ),
        name="composites",
    )(mats)


def turned_kernel(
    points, scale, first_ref, srcs_ref, mats_ref, local_ref, strength_ref, shift_ref, _, high_ref, low_ref, turned_ref, weight_ref
):
    orbs = first_ref.shape[1]
    here = lax.axis_index("energy")
    for offset in range(points):
        total = jnp.float32(0.0)
        for mode in range(strength_ref.shape[0]):
            taken = lax.rem(here + shift_ref[mode], points) == lax.rem(here + points - offset, points)
            total = total + jnp.where(taken, strength_ref[mode], 0.0)
        weight_ref[offset : offset + 1, :] = jnp.full((1, orbs), total * scale, F32)
    for k in range(mats_ref.shape[0] + 1):
        columns = slice(k * orbs, (k + 1) * orbs)
        matrix = first_ref[0] if k == 0 else mats_ref[k - 1]
        local = srcs_ref[:orbs, :] if k == 0 else local_ref[k - 1]
        high_ref[:, columns], low_ref[:, columns] = split(matrix.T)
        turned_ref[:, columns] = local.T


def turned_blocks(mats, srcs, middle, local, strength, shift, after, points, scale):
    count, orbs, _ = mats.shape
    width = srcs.shape[1]
    length = (count - 1) * orbs
    shape = jax.ShapeDtypeStruct((orbs, length), BF16)
    return pl.pallas_call(
        functools.partial(turned_kernel, points, scale),
        out_shape=(
            shape,
            shape,
            jax.ShapeDtypeStruct((width, length), F32),
            jax.ShapeDtypeStruct((points, orbs), F32),
        ),
        in_specs=[VMEM, VMEM, VMEM, VMEM, SMEM, SMEM, VMEM],
        out_specs=(VMEM,) * 4,
        compiler_params=PARAMS,
        name="turned_blocks",
    )(mats, srcs, middle, local, strength, shift, after)


def relay_kernel(step, first, high_ref, low_ref, offset_ref, got_ref, _, *rest):
    out_ref, kept_ref = rest[-2:]
    got = got_ref[...]
    out_ref[...] = product_rows(got, high_ref[...], low_ref[...]) + offset_ref[...]
    other = 0.0 if first else rest[0][...]
    kept_ref[...] = jnp.where(lax.axis_index("cuts") == step, got, other)


def relay(step, last, offset, got, incoming, after):
    shape = jax.ShapeDtypeStruct(got.shape, F32)
    args = [*last, offset, got, after] + ([] if incoming is None else [incoming])
    return pl.pallas_call(
        functools.partial(relay_kernel, step, incoming is None),
        out_shape=(shape, shape),
        in_specs=[VMEM] * len(args),
        out_specs=(VMEM, VMEM),
        compiler_params=PARAMS,
        name="relay",
    )(*args)


def green_kernel(
    step, piece, high_ref, low_ref, turned_ref, last_high_ref, last_low_ref, offset_ref, got_ref, incoming_ref, *rest
):
    green_ref, sums_ref = rest[-2:]
    height, orbs = got_ref.shape
    length = high_ref.shape[1]
    rows = slice(piece * height, (piece + 1) * height)
    state = jnp.where(lax.axis_index("cuts") == step, got_ref[...], incoming_ref[...])
    sums = [jnp.sum(state * state, axis=0, keepdims=True)]
    green = product_rows(state, high_ref[...], low_ref[...]) + turned_ref[rows, :]
    green_ref[:, :length] = green
    for k in range(length // orbs):
        block = green[:, k * orbs : (k + 1) * orbs]
        sums.append(jnp.sum(block * block, axis=0, keepdims=True))
    block = product_rows(state, last_high_ref[...], last_low_ref[...]) + offset_ref[...]
    green_ref[:, length:] = block
    sums.append(jnp.sum(block * block, axis=0, keepdims=True))
    total = jnp.concatenate(sums, axis=0)
    sums_ref[...] = total if len(rest) == 2 else total + rest[0][...]


def green_piece(step, piece, blocks, last, offset, got, incoming, sums):
    height, orbs = got.shape
    count = blocks[0].shape[1] // orbs + 1
    args = [*blocks, *last, offset, got, incoming] + ([] if sums is None else [sums])
    return pl.pallas_call(
        functools.partial(green_kernel, step, piece),
        out_shape=(
            jax.ShapeDtypeStruct((height, count * orbs), F32),
            jax.ShapeDtypeStruct((count + 1, orbs), F32),
        ),
        in_specs=[VMEM] * len(args),
        out_specs=(VMEM, VMEM),
        compiler_params=PARAMS,
        name="green_piece",
    )(*args)


def inner_kernel(coupling_ref, *rest):
    green_refs, (inner_ref, turned_ref) = rest[:-2], rest[-2:]
    orbs = coupling_ref.shape[0]
    coupling = coupling_ref[...]
    green = jnp.concatenate([g[...] for g in green_refs], axis=0)
    low = green.astype(BF16)
    for k in range(low.shape[1] // orbs):
        columns = slice(k * orbs, (k + 1) * orbs)
        inner_ref[:, columns] = dot(low[:, columns], coupling)
        turned_ref[columns, :] = green[:, columns].T


def inner_blocks(coupling, pieces):
    height, length = pieces[0].shape
    width = height * len(pieces)
    return pl.pallas_call(
        inner_kernel,
        out_shape=(
            jax.ShapeDtypeStruct((width, length), F32),
            jax.ShapeDtypeStruct((length, width), F32),
        ),
        in_specs=[VMEM] * (1 + len(pieces)),
        out_specs=(VMEM, VMEM),
        compiler_params=PARAMS,
        cost_estimate=pl.CostEstimate(
            flops=2 * width * length * coupling.shape[0], bytes_accessed=12 * width * length, transcendentals=0
        ),
        name="inner_blocks",
    )(coupling, *pieces)


def scatter_kernel(coupling_ref, inner_ref, green_ref, *rest):
    mixed_ref, *after_refs, out_ref, kept_ref, staged, sems, kept_sem = rest
    kept_copy = pltpu.make_async_copy(green_ref, kept_ref, kept_sem)
    kept_copy.start()
    orbs = coupling_ref.shape[0]
    count = inner_ref.shape[1] // orbs
    here = lax.axis_index("cuts")
    after = jnp.where(lax.rem(here, 2) == 0, after_refs[0][1:2, :], after_refs[1][1:2, :])
    rows = [mixed_ref[k : k + 1, :] for k in range(count + 1)]
    rows.append(jnp.where(here == lax.axis_size("cuts") - 1, 0.0, after))
    coupling = coupling_ref[...]
    copies = []
    for k in range(count):
        selfen = rows[k + 1] + 0.5 * (rows[k] + rows[k + 2])
        columns = slice(k * orbs, (k + 1) * orbs)
        scaled = (inner_ref[:, columns] * selfen).astype(BF16)
        staged[columns, :] = dot_t(coupling, scaled)
        copies.append(pltpu.make_async_copy(staged.at[columns], out_ref.at[columns], sems.at[k]))
        copies[-1].start()
    for copy in copies:
        copy.wait()
    kept_copy.wait()


def scatter_blocks(coupling, inner, green, mixed, after):
    width, length = inner.shape
    orbs = coupling.shape[0]
    shape = jax.ShapeDtypeStruct((length, width), F32)
    return pl.pallas_call(
        scatter_kernel,
        out_shape=(shape, shape),
        in_specs=[VMEM] * (4 + len(after)),
        out_specs=(HBM, HBM),
        scratch_shapes=[
            pltpu.VMEM((length, width), F32),
            pltpu.SemaphoreType.DMA((length // orbs,)),
            pltpu.SemaphoreType.DMA,
        ],
        compiler_params=PARAMS,
        name="scatter_blocks",
    )(coupling, inner, green, mixed, *after)


def paired(lower, cuts, group):
    pairs = []
    for c in range(cuts):
        for g in range(group):
            if c in lower:
                to = (c + 1, g)
            elif c - 1 in lower:
                to = (c - 1, g)
            else:
                to = (c, g ^ 1 if g ^ 1 < group else g)
            pairs.append((c * group + g, to[0] * group + to[1]))
    return pairs


def turned_round(value, axis, offset):
    devices = lax.axis_size(axis)
    return lax.ppermute(value, axis, [(i, (i + offset) % devices) for i in range(devices)])


def body(transfer, source, coupling, strength, mode_shift):
    mats, srcs = transfer[0], source[0]
    width = srcs.shape[1]
    cuts, group, points = (lax.axis_size(a) for a in ("cuts", "group", "energy"))
    pieces = PIECES if width % (8 * PIECES) == 0 else 1
    local, offsets = local_chain(mats, srcs, pieces)
    middle, *last = composites(mats)
    leaving, incoming, blocks = offsets, [None] * pieces, None
    for step in range(1, cuts):
        pairs = paired([step - 1], cuts, group)
        got = [lax.ppermute(piece, ("cuts", "group"), pairs) for piece in leaving]
        if step < cuts - 1:
            leaving, after = [], last[0] if blocks is None else weights
            for piece in range(pieces):
                after, incoming[piece] = relay(
                    step, last, offsets[piece], got[piece], incoming[piece], after
                )
                leaving.append(after)
        if blocks is None:
            *blocks, weights = turned_blocks(
                mats, srcs, middle, local, strength, mode_shift, leaving[-1], points, 1.0 / (width * group)
            )
    green, sums = [], None
    for piece in range(pieces):
        part, sums = green_piece(
            cuts - 1, piece, blocks, last, offsets[piece], got[piece], incoming[piece], sums
        )
        green.append(part)

    parts = [turned_round(sums, "group", k) for k in range(1, group)]
    total = sums + sum(parts)
    inner, kept = inner_blocks(coupling, green)
    mixed = total * weights[:1]
    for k in range(1, points):
        mixed = mixed + turned_round(total, "energy", k) * weights[k : k + 1]
    after = [
        lax.ppermute(mixed, ("cuts", "group"), paired(range(first, cuts - 1, 2), cuts, group))
        for first in (0, 1)
    ]
    scattered, kept = scatter_blocks(coupling, inner, kept, mixed, after)
    return kept[None], scattered[None]


def solution(mesh):
    in_specs = (P("energy", "cuts", None, None), P("energy", "cuts", "group"), P(), P(), P())
    out_specs = (P("energy", "cuts", "group"), P("energy", "cuts", "group"))
    return jax.shard_map(body, mesh=mesh, in_specs=in_specs, out_specs=out_specs, check_vma=False)
```

```python
import functools

import jax
import jax.numpy as jnp
from jax import lax
from jax.experimental import pallas as pl
from jax.experimental.pallas import tpu as pltpu
from jax.sharding import PartitionSpec as P

F32 = jnp.float32
BF16 = jnp.bfloat16
VMEM = pl.BlockSpec(memory_space=pltpu.VMEM)
SMEM = pl.BlockSpec(memory_space=pltpu.SMEM)
HBM = pl.BlockSpec(memory_space=pltpu.HBM)
PARAMS = pltpu.CompilerParams(vmem_limit_bytes=32 * 1024 * 1024)
WHOLE = pltpu.CompilerParams(vmem_limit_bytes=53 * 1024 * 1024)
PIECES = 2


def split(value):
    high = value.astype(BF16)
    return high, (value - high.astype(F32)).astype(BF16)


def dot(left, right):
    return jnp.dot(left, right, preferred_element_type=F32)


def dot_t(left, right):
    return lax.dot_general(left, right, (((1,), (1,)), ((), ())), preferred_element_type=F32)


def product(left_high, left_low, state):
    high, low = split(state)
    width = state.shape[1]
    both = dot(left_high, jnp.concatenate([high, low], axis=1))
    return both[:, :width] + (both[:, width:] + dot(left_low, high))


def product_rows(state, right_high, right_low):
    high, low = split(state)
    height = state.shape[0]
    both = dot(jnp.concatenate([high, low], axis=0), right_high)
    return both[:height] + (both[height:] + dot(high, right_low))


def chain_step(matrix, state, srcs):
    return product(*split(matrix), state) + srcs


def store_pieces(refs, state):
    turned = state.T
    height = turned.shape[0] // len(refs)
    for piece, ref in enumerate(refs):
        ref[...] = turned[piece * height : (piece + 1) * height, :]


def first_kernel(mats_ref, srcs_ref, *rest):
    leaving_refs, (mats, srcs, sems, src_sem) = rest[:-4], rest[-4:]
    count, orbs = mats_ref.shape[0], mats_ref.shape[1]
    first = lax.axis_index("cuts") == 0

    @pl.when(first)
    def _():
        src_copy = pltpu.make_async_copy(srcs_ref, srcs, src_sem)
        copies = [
            pltpu.make_async_copy(mats_ref.at[k], mats.at[k], sems.at[k]) for k in range(1, count)
        ]
        src_copy.start()
        for copy in copies:
            copy.start()
        src_copy.wait()
        state = srcs[:orbs, :]
        for k in range(1, count):
            copies[k - 1].wait()
            state = chain_step(mats[k], state, srcs[k * orbs : (k + 1) * orbs, :])
        store_pieces(leaving_refs, state)

    @pl.when(jnp.logical_not(first))
    def _():
        for ref in leaving_refs:
            ref[...] = jnp.zeros_like(ref)


def first_chain(mats, srcs, pieces):
    count, orbs, _ = mats.shape
    width = srcs.shape[1]
    leaving = jax.ShapeDtypeStruct((width // pieces, orbs), F32)
    return list(
        pl.pallas_call(
            first_kernel,
            out_shape=(leaving,) * pieces,
            in_specs=[HBM, HBM],
            out_specs=(VMEM,) * pieces,
            scratch_shapes=[
                pltpu.VMEM(mats.shape, F32),
                pltpu.VMEM(srcs.shape, F32),
                pltpu.SemaphoreType.DMA((count,)),
                pltpu.SemaphoreType.DMA,
            ],
            compiler_params=WHOLE,
            name="first_chain",
        )(mats, srcs)
    )


def composite_kernel(mats_ref, srcs_ref, middle_ref, local_ref, high_ref, low_ref, *offset_refs):
    full = mats_ref[0]
    count, orbs = mats_ref.shape[0], mats_ref.shape[1]
    state = srcs_ref[:orbs, :]
    for k in range(1, count):
        left_high, left_low = split(mats_ref[k])
        state = product(left_high, left_low, state) + srcs_ref[k * orbs : (k + 1) * orbs, :]
        high, low = split(full)
        full = dot(left_high, high) + (dot(left_high, low) + dot(left_low, high))
        if k < count - 1:
            middle_ref[k - 1] = full
            local_ref[k - 1] = state
    store_pieces(offset_refs, state)
    high_ref[...], low_ref[...] = split(full.T)


def composites(mats, srcs, pieces):
    count, orbs, _ = mats.shape
    width = srcs.shape[1]
    shape = jax.ShapeDtypeStruct((orbs, orbs), BF16)
    outs = pl.pallas_call(
        composite_kernel,
        out_shape=(
            jax.ShapeDtypeStruct((count - 2, orbs, orbs), F32),
            jax.ShapeDtypeStruct((count - 2, orbs, width), F32),
            shape,
            shape,
        )
        + (jax.ShapeDtypeStruct((width // pieces, orbs), F32),) * pieces,
        in_specs=[VMEM, VMEM],
        out_specs=(VMEM,) * (4 + pieces),
        compiler_params=PARAMS,
        cost_estimate=pl.CostEstimate(
            flops=6 * (count - 1) * orbs**3, bytes_accessed=8 * count * orbs**2, transcendentals=0
        ),
        name="composites",
    )(mats, srcs)
    return outs[0], outs[1], outs[2:4], list(outs[4:])


def turned_kernel(
    points, scale, first_ref, srcs_ref, mats_ref, local_ref, strength_ref, shift_ref, _, high_ref, low_ref, turned_ref, weight_ref
):
    orbs = first_ref.shape[1]
    here = lax.axis_index("energy")
    for offset in range(points):
        total = jnp.float32(0.0)
        for mode in range(strength_ref.shape[0]):
            taken = lax.rem(here + shift_ref[mode], points) == lax.rem(here + points - offset, points)
            total = total + jnp.where(taken, strength_ref[mode], 0.0)
        weight_ref[offset : offset + 1, :] = jnp.full((1, orbs), total * scale, F32)
    for k in range(mats_ref.shape[0] + 1):
        columns = slice(k * orbs, (k + 1) * orbs)
        matrix = first_ref[0] if k == 0 else mats_ref[k - 1]
        local = srcs_ref[:orbs, :] if k == 0 else local_ref[k - 1]
        high_ref[:, columns], low_ref[:, columns] = split(matrix.T)
        turned_ref[:, columns] = local.T


def turned_blocks(mats, srcs, middle, local, strength, shift, after, points, scale):
    count, orbs, _ = mats.shape
    width = srcs.shape[1]
    length = (count - 1) * orbs
    shape = jax.ShapeDtypeStruct((orbs, length), BF16)
    return pl.pallas_call(
        functools.partial(turned_kernel, points, scale),
        out_shape=(
            shape,
            shape,
            jax.ShapeDtypeStruct((width, length), F32),
            jax.ShapeDtypeStruct((points, orbs), F32),
        ),
        in_specs=[VMEM, VMEM, VMEM, VMEM, SMEM, SMEM, VMEM],
        out_specs=(VMEM,) * 4,
        compiler_params=PARAMS,
        name="turned_blocks",
    )(mats, srcs, middle, local, strength, shift, after)


def relay_kernel(step, first, high_ref, low_ref, offset_ref, got_ref, _, *rest):
    out_ref, kept_ref = rest[-2:]
    got = got_ref[...]
    out_ref[...] = product_rows(got, high_ref[...], low_ref[...]) + offset_ref[...]
    other = 0.0 if first else rest[0][...]
    kept_ref[...] = jnp.where(lax.axis_index("cuts") == step, got, other)


def relay(step, last, offset, got, incoming, after):
    shape = jax.ShapeDtypeStruct(got.shape, F32)
    args = [*last, offset, got, after] + ([] if incoming is None else [incoming])
    return pl.pallas_call(
        functools.partial(relay_kernel, step, incoming is None),
        out_shape=(shape, shape),
        in_specs=[VMEM] * len(args),
        out_specs=(VMEM, VMEM),
        compiler_params=PARAMS,
        name="relay",
    )(*args)


def green_kernel(
    step, piece, high_ref, low_ref, turned_ref, last_high_ref, last_low_ref, offset_ref, got_ref, incoming_ref, *rest
):
    green_ref, sums_ref = rest[-2:]
    height, orbs = got_ref.shape
    length = high_ref.shape[1]
    rows = slice(piece * height, (piece + 1) * height)
    state = jnp.where(lax.axis_index("cuts") == step, got_ref[...], incoming_ref[...])
    sums = [jnp.sum(state * state, axis=0, keepdims=True)]
    green = product_rows(state, high_ref[...], low_ref[...]) + turned_ref[rows, :]
    green_ref[:, :length] = green
    for k in range(length // orbs):
        block = green[:, k * orbs : (k + 1) * orbs]
        sums.append(jnp.sum(block * block, axis=0, keepdims=True))
    block = product_rows(state, last_high_ref[...], last_low_ref[...]) + offset_ref[...]
    green_ref[:, length:] = block
    sums.append(jnp.sum(block * block, axis=0, keepdims=True))
    total = jnp.concatenate(sums, axis=0)
    sums_ref[...] = total if len(rest) == 2 else total + rest[0][...]


def green_piece(step, piece, blocks, last, offset, got, incoming, sums):
    height, orbs = got.shape
    count = blocks[0].shape[1] // orbs + 1
    args = [*blocks, *last, offset, got, incoming] + ([] if sums is None else [sums])
    return pl.pallas_call(
        functools.partial(green_kernel, step, piece),
        out_shape=(
            jax.ShapeDtypeStruct((height, count * orbs), F32),
            jax.ShapeDtypeStruct((count + 1, orbs), F32),
        ),
        in_specs=[VMEM] * len(args),
        out_specs=(VMEM, VMEM),
        compiler_params=PARAMS,
        name="green_piece",
    )(*args)


def inner_kernel(coupling_ref, *rest):
    green_refs, (inner_ref, turned_ref) = rest[:-2], rest[-2:]
    orbs = coupling_ref.shape[0]
    coupling = coupling_ref[...]
    green = jnp.concatenate([g[...] for g in green_refs], axis=0)
    low = green.astype(BF16)
    for k in range(low.shape[1] // orbs):
        columns = slice(k * orbs, (k + 1) * orbs)
        inner_ref[:, columns] = dot(low[:, columns], coupling)
        turned_ref[columns, :] = green[:, columns].T


def inner_blocks(coupling, pieces):
    height, length = pieces[0].shape
    width = height * len(pieces)
    return pl.pallas_call(
        inner_kernel,
        out_shape=(
            jax.ShapeDtypeStruct((width, length), F32),
            jax.ShapeDtypeStruct((length, width), F32),
        ),
        in_specs=[VMEM] * (1 + len(pieces)),
        out_specs=(VMEM, VMEM),
        compiler_params=PARAMS,
        cost_estimate=pl.CostEstimate(
            flops=2 * width * length * coupling.shape[0], bytes_accessed=12 * width * length, transcendentals=0
        ),
        name="inner_blocks",
    )(coupling, *pieces)


def scatter_kernel(coupling_ref, inner_ref, green_ref, *rest):
    mixed_ref, *after_refs, out_ref, kept_ref, staged, sems, kept_sem = rest
    kept_copy = pltpu.make_async_copy(green_ref, kept_ref, kept_sem)
    kept_copy.start()
    orbs = coupling_ref.shape[0]
    count = inner_ref.shape[1] // orbs
    here = lax.axis_index("cuts")
    after = jnp.where(lax.rem(here, 2) == 1, after_refs[0][1:2, :], after_refs[1][1:2, :])
    rows = [mixed_ref[k : k + 1, :] for k in range(count + 1)]
    rows.append(jnp.where(here == lax.axis_size("cuts") - 1, 0.0, after))
    coupling = coupling_ref[...]
    copies = []
    for k in range(count):
        selfen = rows[k + 1] + 0.5 * (rows[k] + rows[k + 2])
        columns = slice(k * orbs, (k + 1) * orbs)
        scaled = (inner_ref[:, columns] * selfen).astype(BF16)
        staged[columns, :] = dot_t(coupling, scaled)
        copies.append(pltpu.make_async_copy(staged.at[columns], out_ref.at[columns], sems.at[k]))
        copies[-1].start()
    for copy in copies:
        copy.wait()
    kept_copy.wait()


def scatter_blocks(coupling, inner, green, mixed, after):
    width, length = inner.shape
    orbs = coupling.shape[0]
    shape = jax.ShapeDtypeStruct((length, width), F32)
    return pl.pallas_call(
        scatter_kernel,
        out_shape=(shape, shape),
        in_specs=[VMEM] * (4 + len(after)),
        out_specs=(HBM, HBM),
        scratch_shapes=[
            pltpu.VMEM((length, width), F32),
            pltpu.SemaphoreType.DMA((length // orbs,)),
            pltpu.SemaphoreType.DMA,
        ],
        compiler_params=PARAMS,
        name="scatter_blocks",
    )(coupling, inner, green, mixed, *after)


def paired(lower, cuts, group, other=0):
    pairs = []
    for c in range(cuts):
        for g in range(group):
            if c in lower:
                to = (c + 1, g ^ other)
            elif c - 1 in lower:
                to = (c - 1, g ^ other)
            else:
                to = (c, g ^ 1 if g ^ 1 < group else g)
            pairs.append((c * group + g, to[0] * group + to[1]))
    return pairs


def one_way(lower, cuts, group):
    return [(lower * group + g, (lower + 1) * group + g) for g in range(group)]


def across(value, energy, group):
    points, members = lax.axis_size("energy"), lax.axis_size("group")
    pairs = [
        (e * members + g, (e + energy) % points * members + (g ^ group))
        for e in range(points)
        for g in range(members)
    ]
    return lax.ppermute(value, ("energy", "group"), pairs)


def body(transfer, source, coupling, strength, mode_shift):
    mats, srcs = transfer[0], source[0]
    width = srcs.shape[1]
    cuts, group, points = (lax.axis_size(a) for a in ("cuts", "group", "energy"))
    pieces = PIECES if width % (8 * PIECES) == 0 else 1
    leaving = first_chain(mats, srcs, pieces)
    middle, local, last, offsets = composites(mats, srcs, pieces)
    incoming = [None] * pieces
    for step in range(1, cuts):
        if step < cuts - 1:
            pairs = paired([step - 1], cuts, group)
        else:
            pairs = one_way(step - 1, cuts, group)
        got = [lax.ppermute(piece, ("cuts", "group"), pairs) for piece in leaving]
        if step < cuts - 1:
            leaving, after = [], last[0]
            for piece in range(pieces):
                after, incoming[piece] = relay(
                    step, last, offsets[piece], got[piece], incoming[piece], after
                )
                leaving.append(after)
    *blocks, weights = turned_blocks(
        mats, srcs, middle, local, strength, mode_shift, leaving[-1], points, 1.0 / (width * group)
    )
    green, sums = [], None
    for piece in range(pieces):
        part, sums = green_piece(
            cuts - 1, piece, blocks, last, offsets[piece], got[piece], incoming[piece], sums
        )
        green.append(part)

    sums = sums + sum(across(sums, 0, k) for k in range(1, group))
    other = 1 if group % 2 == 0 else 0
    mixed = sums * weights[:1]
    for offset in range(1, points):
        mixed = mixed + across(sums, offset, other) * weights[offset : offset + 1]
    inner, kept = inner_blocks(coupling, green)
    after = [
        lax.ppermute(
            mixed, ("cuts", "group"), paired(range(first, cuts - 1, 2), cuts, group, other)
        )
        for first in (1, 0)
    ]
    scattered, kept = scatter_blocks(coupling, inner, kept, mixed, after)
    return kept[None], scattered[None]


def solution(mesh):
    in_specs = (P("energy", "cuts", None, None), P("energy", "cuts", "group"), P(), P(), P())
    out_specs = (P("energy", "cuts", "group"), P("energy", "cuts", "group"))
    return jax.shard_map(body, mesh=mesh, in_specs=in_specs, out_specs=out_specs, check_vma=False)
```

```python
import functools

import jax
import jax.numpy as jnp
from jax import lax
from jax.experimental import pallas as pl
from jax.experimental.pallas import tpu as pltpu
from jax.sharding import PartitionSpec as P

F32 = jnp.float32
BF16 = jnp.bfloat16
VMEM = pl.BlockSpec(memory_space=pltpu.VMEM)
SMEM = pl.BlockSpec(memory_space=pltpu.SMEM)
HBM = pl.BlockSpec(memory_space=pltpu.HBM)
PARAMS = pltpu.CompilerParams(vmem_limit_bytes=32 * 1024 * 1024)
WHOLE = pltpu.CompilerParams(vmem_limit_bytes=107 * 512 * 1024)
SHARES = (9, 7)


def split(value):
    high = value.astype(BF16)
    return high, (value - high.astype(F32)).astype(BF16)


def dot(left, right):
    return jnp.dot(left, right, preferred_element_type=F32)


def dot_t(left, right):
    return lax.dot_general(left, right, (((1,), (1,)), ((), ())), preferred_element_type=F32)


def product(left_high, left_low, state):
    high, low = split(state)
    width = state.shape[1]
    both = dot(left_high, jnp.concatenate([high, low], axis=1))
    return both[:, :width] + (both[:, width:] + dot(left_low, high))


def product_rows(state, right_high, right_low):
    high, low = split(state)
    height = state.shape[0]
    both = dot(jnp.concatenate([high, low], axis=0), right_high)
    return both[:height] + (both[height:] + dot(high, right_low))


def chain_step(matrix, state, srcs):
    return product(*split(matrix), state) + srcs


def heights_of(width):
    if width % 8 or width // 8 < sum(SHARES):
        return (width,)
    ends = [8 * (width // 8 * sum(SHARES[: k + 1]) // sum(SHARES)) for k in range(len(SHARES))]
    return tuple(end - start for start, end in zip([0, *ends], ends))


def store_pieces(refs, state):
    turned = state.T
    start = 0
    for ref in refs:
        ref[...] = turned[start : start + ref.shape[0], :]
        start += ref.shape[0]


def first_kernel(mats_ref, srcs_ref, *rest):
    leaving_refs, (mats, srcs, sems, src_sem) = rest[:-4], rest[-4:]
    count, orbs = mats_ref.shape[0], mats_ref.shape[1]
    first = lax.axis_index("cuts") == 0

    @pl.when(first)
    def _():
        src_copy = pltpu.make_async_copy(srcs_ref, srcs, src_sem)
        copies = [
            pltpu.make_async_copy(mats_ref.at[k], mats.at[k], sems.at[k]) for k in range(1, count)
        ]
        src_copy.start()
        for copy in copies:
            copy.start()
        src_copy.wait()
        state = srcs[:orbs, :]
        for k in range(1, count):
            copies[k - 1].wait()
            state = chain_step(mats[k], state, srcs[k * orbs : (k + 1) * orbs, :])
        store_pieces(leaving_refs, state)

    @pl.when(jnp.logical_not(first))
    def _():
        for ref in leaving_refs:
            ref[...] = jnp.zeros_like(ref)


def first_chain(mats, srcs, heights):
    count, orbs, _ = mats.shape
    return list(
        pl.pallas_call(
            first_kernel,
            out_shape=tuple(jax.ShapeDtypeStruct((height, orbs), F32) for height in heights),
            in_specs=[HBM, HBM],
            out_specs=(VMEM,) * len(heights),
            scratch_shapes=[
                pltpu.VMEM(mats.shape, F32),
                pltpu.VMEM(srcs.shape, F32),
                pltpu.SemaphoreType.DMA((count,)),
                pltpu.SemaphoreType.DMA,
            ],
            compiler_params=WHOLE,
            name="first_chain",
        )(mats, srcs)
    )


def composite_kernel(mats_ref, srcs_ref, middle_ref, local_ref, high_ref, low_ref, *offset_refs):
    full = mats_ref[0]
    count, orbs = mats_ref.shape[0], mats_ref.shape[1]
    state = srcs_ref[:orbs, :]
    for k in range(1, count):
        left_high, left_low = split(mats_ref[k])
        state = product(left_high, left_low, state) + srcs_ref[k * orbs : (k + 1) * orbs, :]
        high, low = split(full)
        full = dot(left_high, high) + (dot(left_high, low) + dot(left_low, high))
        if k < count - 1:
            middle_ref[k - 1] = full
            local_ref[k - 1] = state
    store_pieces(offset_refs, state)
    high_ref[...], low_ref[...] = split(full.T)


def composites(mats, srcs, heights):
    count, orbs, _ = mats.shape
    width = srcs.shape[1]
    shape = jax.ShapeDtypeStruct((orbs, orbs), BF16)
    outs = pl.pallas_call(
        composite_kernel,
        out_shape=(
            jax.ShapeDtypeStruct((count - 2, orbs, orbs), F32),
            jax.ShapeDtypeStruct((count - 2, orbs, width), F32),
            shape,
            shape,
        )
        + tuple(jax.ShapeDtypeStruct((height, orbs), F32) for height in heights),
        in_specs=[VMEM, VMEM],
        out_specs=(VMEM,) * (4 + len(heights)),
        compiler_params=PARAMS,
        cost_estimate=pl.CostEstimate(
            flops=6 * (count - 1) * orbs**3, bytes_accessed=8 * count * orbs**2, transcendentals=0
        ),
        name="composites",
    )(mats, srcs)
    return outs[0], outs[1], outs[2:4], list(outs[4:])


def turned_kernel(
    points, scale, first_ref, srcs_ref, mats_ref, local_ref, strength_ref, shift_ref, _, high_ref, low_ref, turned_ref, weight_ref
):
    orbs = first_ref.shape[1]
    here = lax.axis_index("energy")
    for offset in range(points):
        total = jnp.float32(0.0)
        for mode in range(strength_ref.shape[0]):
            taken = lax.rem(here + shift_ref[mode], points) == lax.rem(here + points - offset, points)
            total = total + jnp.where(taken, strength_ref[mode], 0.0)
        weight_ref[offset : offset + 1, :] = jnp.full((1, orbs), total * scale, F32)
    for k in range(mats_ref.shape[0] + 1):
        columns = slice(k * orbs, (k + 1) * orbs)
        matrix = first_ref[0] if k == 0 else mats_ref[k - 1]
        local = srcs_ref[:orbs, :] if k == 0 else local_ref[k - 1]
        high_ref[:, columns], low_ref[:, columns] = split(matrix.T)
        turned_ref[:, columns] = local.T


def turned_blocks(mats, srcs, middle, local, strength, shift, after, points, scale):
    count, orbs, _ = mats.shape
    width = srcs.shape[1]
    length = (count - 1) * orbs
    shape = jax.ShapeDtypeStruct((orbs, length), BF16)
    return pl.pallas_call(
        functools.partial(turned_kernel, points, scale),
        out_shape=(
            shape,
            shape,
            jax.ShapeDtypeStruct((width, length), F32),
            jax.ShapeDtypeStruct((points, orbs), F32),
        ),
        in_specs=[VMEM, VMEM, VMEM, VMEM, SMEM, SMEM, VMEM],
        out_specs=(VMEM,) * 4,
        compiler_params=PARAMS,
        name="turned_blocks",
    )(mats, srcs, middle, local, strength, shift, after)


def relay_kernel(step, first, high_ref, low_ref, offset_ref, got_ref, _, *rest):
    out_ref, kept_ref = rest[-2:]
    got = got_ref[...]
    out_ref[...] = product_rows(got, high_ref[...], low_ref[...]) + offset_ref[...]
    other = 0.0 if first else rest[0][...]
    kept_ref[...] = jnp.where(lax.axis_index("cuts") == step, got, other)


def relay(step, last, offset, got, incoming, after):
    shape = jax.ShapeDtypeStruct(got.shape, F32)
    args = [*last, offset, got, after] + ([] if incoming is None else [incoming])
    return pl.pallas_call(
        functools.partial(relay_kernel, step, incoming is None),
        out_shape=(shape, shape),
        in_specs=[VMEM] * len(args),
        out_specs=(VMEM, VMEM),
        compiler_params=PARAMS,
        name="relay",
    )(*args)


def green_kernel(
    step, start, high_ref, low_ref, turned_ref, last_high_ref, last_low_ref, offset_ref, got_ref, incoming_ref, *rest
):
    green_ref, sums_ref = rest[-2:]
    height, orbs = got_ref.shape
    length = high_ref.shape[1]
    rows = slice(start, start + height)
    state = jnp.where(lax.axis_index("cuts") == step, got_ref[...], incoming_ref[...])
    sums = [jnp.sum(state * state, axis=0, keepdims=True)]
    green = product_rows(state, high_ref[...], low_ref[...]) + turned_ref[rows, :]
    green_ref[:, :length] = green
    for k in range(length // orbs):
        block = green[:, k * orbs : (k + 1) * orbs]
        sums.append(jnp.sum(block * block, axis=0, keepdims=True))
    block = product_rows(state, last_high_ref[...], last_low_ref[...]) + offset_ref[...]
    green_ref[:, length:] = block
    sums.append(jnp.sum(block * block, axis=0, keepdims=True))
    total = jnp.concatenate(sums, axis=0)
    sums_ref[...] = total if len(rest) == 2 else total + rest[0][...]


def green_piece(step, start, blocks, last, offset, got, incoming, sums):
    height, orbs = got.shape
    count = blocks[0].shape[1] // orbs + 1
    args = [*blocks, *last, offset, got, incoming] + ([] if sums is None else [sums])
    return pl.pallas_call(
        functools.partial(green_kernel, step, start),
        out_shape=(
            jax.ShapeDtypeStruct((height, count * orbs), F32),
            jax.ShapeDtypeStruct((count + 1, orbs), F32),
        ),
        in_specs=[VMEM] * len(args),
        out_specs=(VMEM, VMEM),
        compiler_params=PARAMS,
        name="green_piece",
    )(*args)


def inner_kernel(coupling_ref, *rest):
    green_refs, (inner_ref, turned_ref) = rest[:-2], rest[-2:]
    orbs = coupling_ref.shape[0]
    coupling = coupling_ref[...]
    green = jnp.concatenate([g[...] for g in green_refs], axis=0)
    low = green.astype(BF16)
    for k in range(low.shape[1] // orbs):
        columns = slice(k * orbs, (k + 1) * orbs)
        inner_ref[:, columns] = dot(low[:, columns], coupling)
        turned_ref[columns, :] = green[:, columns].T


def inner_blocks(coupling, pieces):
    length = pieces[0].shape[1]
    width = sum(piece.shape[0] for piece in pieces)
    return pl.pallas_call(
        inner_kernel,
        out_shape=(
            jax.ShapeDtypeStruct((width, length), F32),
            jax.ShapeDtypeStruct((length, width), F32),
        ),
        in_specs=[VMEM] * (1 + len(pieces)),
        out_specs=(VMEM, VMEM),
        compiler_params=PARAMS,
        cost_estimate=pl.CostEstimate(
            flops=2 * width * length * coupling.shape[0], bytes_accessed=12 * width * length, transcendentals=0
        ),
        name="inner_blocks",
    )(coupling, *pieces)


def smoothed(rows, k):
    return rows[k + 1] + 0.5 * (rows[k] + rows[k + 2])


def scatter_kernel(coupling_ref, inner_ref, green_ref, mixed_ref, out_ref, kept_ref, staged, sems, kept_sem):
    kept_copy = pltpu.make_async_copy(green_ref, kept_ref, kept_sem)
    kept_copy.start()
    orbs = coupling_ref.shape[0]
    count = inner_ref.shape[1] // orbs
    rows = [mixed_ref[k : k + 1, :] for k in range(count + 1)]
    coupling = coupling_ref[...]
    copies = []
    for k in range(count - 1):
        columns = slice(k * orbs, (k + 1) * orbs)
        scaled = (inner_ref[:, columns] * smoothed(rows, k)).astype(BF16)
        staged[columns, :] = dot_t(coupling, scaled)
        copies.append(pltpu.make_async_copy(staged.at[columns], out_ref.at[columns], sems.at[k]))
        copies[-1].start()
    for copy in copies:
        copy.wait()
    kept_copy.wait()


def scatter_blocks(coupling, inner, green, mixed):
    width, length = inner.shape
    orbs = coupling.shape[0]
    shape = jax.ShapeDtypeStruct((length, width), F32)
    return pl.pallas_call(
        scatter_kernel,
        out_shape=(shape, shape),
        in_specs=[VMEM] * 4,
        out_specs=(HBM, HBM),
        scratch_shapes=[
            pltpu.VMEM((length - orbs, width), F32),
            pltpu.SemaphoreType.DMA((length // orbs - 1,)),
            pltpu.SemaphoreType.DMA,
        ],
        compiler_params=PARAMS,
        name="scatter_blocks",
    )(coupling, inner, green, mixed)


def last_kernel(coupling_ref, inner_ref, mixed_ref, _, *rest):
    *after_refs, out_ref, staged, sem = rest
    orbs = coupling_ref.shape[0]
    count = inner_ref.shape[1] // orbs
    here = lax.axis_index("cuts")
    after = jnp.zeros((1, orbs), F32)
    for lower, after_ref in enumerate(after_refs):
        after = jnp.where(here == lower, after_ref[:1, :], after)
    rows = [mixed_ref[k : k + 1, :] for k in range(count + 1)] + [after]
    columns = slice((count - 1) * orbs, count * orbs)
    scaled = (inner_ref[:, columns] * smoothed(rows, count - 1)).astype(BF16)
    staged[...] = dot_t(coupling_ref[...], scaled)
    copy = pltpu.make_async_copy(staged, out_ref.at[columns], sem)
    copy.start()
    copy.wait()


def last_block(coupling, inner, mixed, partial, after):
    orbs = coupling.shape[0]
    return pl.pallas_call(
        last_kernel,
        out_shape=jax.ShapeDtypeStruct(partial.shape, F32),
        in_specs=[VMEM] * 3 + [HBM] + [VMEM] * len(after),
        out_specs=HBM,
        scratch_shapes=[pltpu.VMEM((orbs, partial.shape[1]), F32), pltpu.SemaphoreType.DMA],
        input_output_aliases={3: 0},
        compiler_params=PARAMS,
        name="last_block",
    )(coupling, inner, mixed, partial, *after)


def edge_kernel(mixed_ref, _, *out_refs):
    for out_ref in out_refs:
        out_ref[...] = jnp.broadcast_to(mixed_ref[1:2, :], out_ref.shape)


def edge_rows(mixed, after, cuts):
    return pl.pallas_call(
        edge_kernel,
        out_shape=tuple(
            jax.ShapeDtypeStruct((4 * (cuts - 1 - lower), mixed.shape[1]), F32)
            for lower in range(cuts - 1)
        ),
        in_specs=[VMEM, VMEM],
        out_specs=(VMEM,) * (cuts - 1),
        compiler_params=PARAMS,
        name="edge_rows",
    )(mixed, after)


def paired(lower, cuts, group, other=0):
    pairs = []
    for c in range(cuts):
        for g in range(group):
            if c in lower:
                to = (c + 1, g ^ other)
            elif c - 1 in lower:
                to = (c - 1, g ^ other)
            else:
                to = (c, g ^ 1 if g ^ 1 < group else g)
            pairs.append((c * group + g, to[0] * group + to[1]))
    return pairs


def one_way(lower, cuts, group):
    return [(lower * group + g, (lower + 1) * group + g) for g in range(group)]


def across(value, energy, group):
    points, members = lax.axis_size("energy"), lax.axis_size("group")
    pairs = [
        (e * members + g, (e + energy) % points * members + (g ^ group))
        for e in range(points)
        for g in range(members)
    ]
    return lax.ppermute(value, ("energy", "group"), pairs)


def body(transfer, source, coupling, strength, mode_shift):
    mats, srcs = transfer[0], source[0]
    width = srcs.shape[1]
    cuts, group, points = (lax.axis_size(a) for a in ("cuts", "group", "energy"))
    heights = heights_of(width)
    pieces = len(heights)
    middle, local, last, offsets = composites(mats, srcs, heights)
    leaving = first_chain(mats, srcs, heights[:1]) + offsets[1:]
    incoming, blocks = [None] * pieces, None
    for step in range(1, cuts):
        if step < cuts - 1:
            pairs = paired([step - 1], cuts, group)
        else:
            pairs = one_way(step - 1, cuts, group)
        got = [lax.ppermute(piece, ("cuts", "group"), pairs) for piece in leaving]
        if step < cuts - 1:
            leaving, after = [], last[0] if blocks is None else weights
            for piece in range(pieces):
                after, incoming[piece] = relay(
                    step, last, offsets[piece], got[piece], incoming[piece], after
                )
                leaving.append(after)
        if blocks is None:
            *blocks, weights = turned_blocks(
                mats, srcs, middle, local, strength, mode_shift, leaving[-1], points, 1.0 / (width * group)
            )
    green, sums = [], None
    for piece in range(pieces):
        part, sums = green_piece(
            cuts - 1, sum(heights[:piece]), blocks, last, offsets[piece], got[piece], incoming[piece], sums
        )
        green.append(part)

    other = 1 if group % 2 == 0 else 0
    if other:
        sums = sums + across(sums, 0, 1)
    sums = sums + sum(across(sums, 0, k + other) for k in range(1 + other, group, 1 + other))
    mixed = sums * weights[:1]
    for offset in range(1, points):
        mixed = mixed + across(sums, offset, other) * weights[offset : offset + 1]
    inner, kept = inner_blocks(coupling, green)
    edges = edge_rows(mixed, inner, cuts)
    after = [
        lax.ppermute(
            edges[lower], ("cuts", "group"), paired([lower], cuts, group, other)
        )
        for lower in range(cuts - 1)
    ]
    partial, kept = scatter_blocks(coupling, inner, kept, mixed)
    scattered = last_block(coupling, inner, mixed, partial, after)
    return kept[None], scattered[None]


def solution(mesh):
    in_specs = (P("energy", "cuts", None, None), P("energy", "cuts", "group"), P(), P(), P())
    out_specs = (P("energy", "cuts", "group"), P("energy", "cuts", "group"))
    return jax.shard_map(body, mesh=mesh, in_specs=in_specs, out_specs=out_specs, check_vma=False)
```

```python
import functools

import jax
import jax.numpy as jnp
from jax import lax
from jax.experimental import pallas as pl
from jax.experimental.pallas import tpu as pltpu
from jax.sharding import PartitionSpec as P

F32 = jnp.float32
BF16 = jnp.bfloat16
VMEM = pl.BlockSpec(memory_space=pltpu.VMEM)
HBM = pl.BlockSpec(memory_space=pltpu.HBM)
PARAMS = pltpu.CompilerParams(vmem_limit_bytes=32 * 1024 * 1024)
WHOLE = pltpu.CompilerParams(vmem_limit_bytes=107 * 512 * 1024)
SHARES = (9, 7)


def split(value):
    high = value.astype(BF16)
    return high, (value - high.astype(F32)).astype(BF16)


def dot(left, right):
    return jnp.dot(left, right, preferred_element_type=F32)


def dot_t(left, right):
    return lax.dot_general(left, right, (((1,), (1,)), ((), ())), preferred_element_type=F32)


def product(left_high, left_low, state):
    high, low = split(state)
    width = state.shape[1]
    both = dot(left_high, jnp.concatenate([high, low], axis=1))
    return both[:, :width] + (both[:, width:] + dot(left_low, high))


def product_rows(state, right_high, right_low):
    high, low = split(state)
    height = state.shape[0]
    both = dot(jnp.concatenate([high, low], axis=0), right_high)
    return both[:height] + (both[height:] + dot(high, right_low))


def chain_step(matrix, state, srcs):
    return product(*split(matrix), state) + srcs


def heights_of(width):
    if width % 8 or width // 8 < sum(SHARES):
        return (width,)
    ends = [8 * (width // 8 * sum(SHARES[: k + 1]) // sum(SHARES)) for k in range(len(SHARES))]
    return tuple(end - start for start, end in zip([0, *ends], ends))


def store_pieces(refs, state):
    turned = state.T
    start = 0
    for ref in refs:
        ref[...] = turned[start : start + ref.shape[0], :]
        start += ref.shape[0]


def first_kernel(mats_ref, srcs_ref, *rest):
    leaving_refs, (mats, srcs, sems, src_sem) = rest[:-4], rest[-4:]
    count, orbs = mats_ref.shape[0], mats_ref.shape[1]
    first = lax.axis_index("cuts") == 0

    @pl.when(first)
    def _():
        src_copy = pltpu.make_async_copy(srcs_ref, srcs, src_sem)
        copies = [
            pltpu.make_async_copy(mats_ref.at[k], mats.at[k], sems.at[k]) for k in range(1, count)
        ]
        src_copy.start()
        for copy in copies:
            copy.start()
        src_copy.wait()
        state = srcs[:orbs, :]
        for k in range(1, count):
            copies[k - 1].wait()
            state = chain_step(mats[k], state, srcs[k * orbs : (k + 1) * orbs, :])
        store_pieces(leaving_refs, state)

    @pl.when(jnp.logical_not(first))
    def _():
        for ref in leaving_refs:
            ref[...] = jnp.zeros_like(ref)


def first_chain(mats, srcs, heights):
    count, orbs, _ = mats.shape
    return list(
        pl.pallas_call(
            first_kernel,
            out_shape=tuple(jax.ShapeDtypeStruct((height, orbs), F32) for height in heights),
            in_specs=[HBM, HBM],
            out_specs=(VMEM,) * len(heights),
            scratch_shapes=[
                pltpu.VMEM(mats.shape, F32),
                pltpu.VMEM(srcs.shape, F32),
                pltpu.SemaphoreType.DMA((count,)),
                pltpu.SemaphoreType.DMA,
            ],
            compiler_params=WHOLE,
            name="first_chain",
        )(mats, srcs)
    )


def composite_kernel(mats_ref, srcs_ref, middle_ref, local_ref, high_ref, low_ref, *offset_refs):
    full = mats_ref[0]
    count, orbs = mats_ref.shape[0], mats_ref.shape[1]
    state = srcs_ref[:orbs, :]
    for k in range(1, count):
        left_high, left_low = split(mats_ref[k])
        state = product(left_high, left_low, state) + srcs_ref[k * orbs : (k + 1) * orbs, :]
        high, low = split(full)
        full = dot(left_high, high) + (dot(left_high, low) + dot(left_low, high))
        if k < count - 1:
            middle_ref[k - 1] = full
            local_ref[k - 1] = state
    store_pieces(offset_refs, state)
    high_ref[...], low_ref[...] = split(full.T)


def composites(mats, srcs, heights):
    count, orbs, _ = mats.shape
    width = srcs.shape[1]
    shape = jax.ShapeDtypeStruct((orbs, orbs), BF16)
    outs = pl.pallas_call(
        composite_kernel,
        out_shape=(
            jax.ShapeDtypeStruct((count - 2, orbs, orbs), F32),
            jax.ShapeDtypeStruct((count - 2, orbs, width), F32),
            shape,
            shape,
        )
        + tuple(jax.ShapeDtypeStruct((height, orbs), F32) for height in heights),
        in_specs=[VMEM, VMEM],
        out_specs=(VMEM,) * (4 + len(heights)),
        compiler_params=PARAMS,
        cost_estimate=pl.CostEstimate(
            flops=6 * (count - 1) * orbs**3, bytes_accessed=8 * count * orbs**2, transcendentals=0
        ),
        name="composites",
    )(mats, srcs)
    return outs[0], outs[1], outs[2:4], list(outs[4:])


def turned_kernel(
    points, scale, first_ref, srcs_ref, mats_ref, local_ref, strength_ref, shift_ref, _, high_ref, low_ref, turned_ref, weight_ref
):
    orbs = first_ref.shape[1]
    here = lax.axis_index("energy")
    goal = here + shift_ref[...]
    goal = jnp.where(goal >= points, goal - points, goal)
    for offset in range(points):
        from_here = lax.rem(here + points - offset, points)
        total = jnp.sum(
            jnp.where(goal == from_here, strength_ref[...], 0.0), axis=1, keepdims=True
        )
        weight_ref[offset : offset + 1, :] = jnp.broadcast_to(total * scale, (1, orbs))
    for k in range(mats_ref.shape[0] + 1):
        columns = slice(k * orbs, (k + 1) * orbs)
        matrix = first_ref[0] if k == 0 else mats_ref[k - 1]
        local = srcs_ref[:orbs, :] if k == 0 else local_ref[k - 1]
        high_ref[:, columns], low_ref[:, columns] = split(matrix.T)
        turned_ref[:, columns] = local.T


def turned_blocks(mats, srcs, middle, local, strength, shift, after, points, scale):
    count, orbs, _ = mats.shape
    width = srcs.shape[1]
    length = (count - 1) * orbs
    shape = jax.ShapeDtypeStruct((orbs, length), BF16)
    return pl.pallas_call(
        functools.partial(turned_kernel, points, scale),
        out_shape=(
            shape,
            shape,
            jax.ShapeDtypeStruct((width, length), F32),
            jax.ShapeDtypeStruct((points, orbs), F32),
        ),
        in_specs=[VMEM] * 7,
        out_specs=(VMEM,) * 4,
        compiler_params=PARAMS,
        name="turned_blocks",
    )(mats, srcs, middle, local, strength, shift, after)


def relay_kernel(step, first, high_ref, low_ref, offset_ref, got_ref, _, *rest):
    out_ref, kept_ref = rest[-2:]
    got = got_ref[...]
    out_ref[...] = product_rows(got, high_ref[...], low_ref[...]) + offset_ref[...]
    other = 0.0 if first else rest[0][...]
    kept_ref[...] = jnp.where(lax.axis_index("cuts") == step, got, other)


def relay(step, last, offset, got, incoming, after):
    shape = jax.ShapeDtypeStruct(got.shape, F32)
    args = [*last, offset, got, after] + ([] if incoming is None else [incoming])
    return pl.pallas_call(
        functools.partial(relay_kernel, step, incoming is None),
        out_shape=(shape, shape),
        in_specs=[VMEM] * len(args),
        out_specs=(VMEM, VMEM),
        compiler_params=PARAMS,
        name="relay",
    )(*args)


def green_kernel(
    step, start, high_ref, low_ref, turned_ref, last_high_ref, last_low_ref, offset_ref, got_ref, incoming_ref, *rest
):
    green_ref, sums_ref = rest[-2:]
    height, orbs = got_ref.shape
    length = high_ref.shape[1]
    rows = slice(start, start + height)
    state = jnp.where(lax.axis_index("cuts") == step, got_ref[...], incoming_ref[...])
    sums = [jnp.sum(state * state, axis=0, keepdims=True)]
    green = product_rows(state, high_ref[...], low_ref[...]) + turned_ref[rows, :]
    green_ref[:, :length] = green
    for k in range(length // orbs):
        block = green[:, k * orbs : (k + 1) * orbs]
        sums.append(jnp.sum(block * block, axis=0, keepdims=True))
    block = product_rows(state, last_high_ref[...], last_low_ref[...]) + offset_ref[...]
    green_ref[:, length:] = block
    sums.append(jnp.sum(block * block, axis=0, keepdims=True))
    total = jnp.concatenate(sums, axis=0)
    sums_ref[...] = total if len(rest) == 2 else total + rest[0][...]


def green_piece(step, start, blocks, last, offset, got, incoming, sums):
    height, orbs = got.shape
    count = blocks[0].shape[1] // orbs + 1
    args = [*blocks, *last, offset, got, incoming] + ([] if sums is None else [sums])
    return pl.pallas_call(
        functools.partial(green_kernel, step, start),
        out_shape=(
            jax.ShapeDtypeStruct((height, count * orbs), F32),
            jax.ShapeDtypeStruct((count + 1, orbs), F32),
        ),
        in_specs=[VMEM] * len(args),
        out_specs=(VMEM, VMEM),
        compiler_params=PARAMS,
        name="green_piece",
    )(*args)


def inner_kernel(coupling_ref, *rest):
    green_refs, (inner_ref, turned_ref) = rest[:-2], rest[-2:]
    orbs = coupling_ref.shape[0]
    coupling = coupling_ref[...]
    green = jnp.concatenate([g[...] for g in green_refs], axis=0)
    low = green.astype(BF16)
    for k in range(low.shape[1] // orbs):
        columns = slice(k * orbs, (k + 1) * orbs)
        inner_ref[:, columns] = dot(low[:, columns], coupling)
        turned_ref[columns, :] = green[:, columns].T


def inner_blocks(coupling, pieces):
    length = pieces[0].shape[1]
    width = sum(piece.shape[0] for piece in pieces)
    return pl.pallas_call(
        inner_kernel,
        out_shape=(
            jax.ShapeDtypeStruct((width, length), F32),
            jax.ShapeDtypeStruct((length, width), F32),
        ),
        in_specs=[VMEM] * (1 + len(pieces)),
        out_specs=(VMEM, VMEM),
        compiler_params=PARAMS,
        cost_estimate=pl.CostEstimate(
            flops=2 * width * length * coupling.shape[0], bytes_accessed=12 * width * length, transcendentals=0
        ),
        name="inner_blocks",
    )(coupling, *pieces)


def smoothed(rows, k):
    return rows[k + 1] + 0.5 * (rows[k] + rows[k + 2])


def scattered_block(coupling, inner_ref, rows, k):
    orbs = coupling.shape[0]
    columns = slice(k * orbs, (k + 1) * orbs)
    return dot_t(coupling, (inner_ref[:, columns] * smoothed(rows, k)).astype(BF16))


def early_kernel(coupling_ref, inner_ref, green_ref, mixed_ref, out_ref, kept_ref, staged, sems, kept_sem):
    kept_copy = pltpu.make_async_copy(green_ref, kept_ref, kept_sem)
    kept_copy.start()
    orbs = coupling_ref.shape[0]
    count = inner_ref.shape[1] // orbs
    coupling = coupling_ref[...]
    rows = [mixed_ref[k : k + 1, :] for k in range(count + 1)]
    rows.append(jnp.zeros_like(rows[0]))
    last = lax.axis_index("cuts") == lax.axis_size("cuts") - 1

    def block_copy(k):
        columns = slice(k * orbs, (k + 1) * orbs)
        return pltpu.make_async_copy(staged.at[columns], out_ref.at[columns], sems.at[k])

    def block_start(k):
        staged[k * orbs : (k + 1) * orbs, :] = scattered_block(coupling, inner_ref, rows, k)
        block_copy(k).start()

    for k in range(count - 1):
        block_start(k)

    @pl.when(last)
    def _():
        block_start(count - 1)

    for k in range(count - 1):
        block_copy(k).wait()

    @pl.when(last)
    def _():
        block_copy(count - 1).wait()

    kept_copy.wait()


def early_blocks(coupling, inner, green, mixed):
    width, length = inner.shape
    orbs = coupling.shape[0]
    shape = jax.ShapeDtypeStruct((length, width), F32)
    return pl.pallas_call(
        early_kernel,
        out_shape=(shape, shape),
        in_specs=[VMEM] * 4,
        out_specs=(HBM, HBM),
        scratch_shapes=[
            pltpu.VMEM((length, width), F32),
            pltpu.SemaphoreType.DMA((length // orbs,)),
            pltpu.SemaphoreType.DMA,
        ],
        compiler_params=PARAMS,
        name="early_blocks",
    )(coupling, inner, green, mixed)


def late_kernel(coupling_ref, inner_ref, mixed_ref, _, *rest):
    *after_refs, out_ref, block, sem = rest
    orbs = coupling_ref.shape[0]
    count = inner_ref.shape[1] // orbs
    here = lax.axis_index("cuts")

    @pl.when(here < lax.axis_size("cuts") - 1)
    def _():
        after = jnp.zeros((1, orbs), F32)
        for lower, after_ref in enumerate(after_refs):
            after = jnp.where(here == lower, after_ref[:1, :], after)
        rows = [mixed_ref[k : k + 1, :] for k in range(count + 1)] + [after]
        block[...] = scattered_block(coupling_ref[...], inner_ref, rows, count - 1)
        copy = pltpu.make_async_copy(block, out_ref.at[slice((count - 1) * orbs, count * orbs)], sem)
        copy.start()
        copy.wait()


def late_blocks(coupling, inner, mixed, out, after):
    orbs = coupling.shape[0]
    return pl.pallas_call(
        late_kernel,
        out_shape=jax.ShapeDtypeStruct(out.shape, F32),
        in_specs=[VMEM] * 3 + [HBM] + [VMEM] * len(after),
        out_specs=HBM,
        scratch_shapes=[pltpu.VMEM((orbs, out.shape[1]), F32), pltpu.SemaphoreType.DMA],
        input_output_aliases={3: 0},
        compiler_params=PARAMS,
        name="late_blocks",
    )(coupling, inner, mixed, out, *after)


def edge_kernel(mixed_ref, _, *out_refs):
    for out_ref in out_refs:
        out_ref[...] = jnp.broadcast_to(mixed_ref[1:2, :], out_ref.shape)


def edge_rows(mixed, after, cuts):
    return pl.pallas_call(
        edge_kernel,
        out_shape=tuple(
            jax.ShapeDtypeStruct((4 * (cuts - 1 - lower), mixed.shape[1]), F32)
            for lower in range(cuts - 1)
        ),
        in_specs=[VMEM, VMEM],
        out_specs=(VMEM,) * (cuts - 1),
        compiler_params=PARAMS,
        name="edge_rows",
    )(mixed, after)


def paired(lower, cuts, group, other=0):
    pairs = []
    for c in range(cuts):
        for g in range(group):
            if c in lower:
                to = (c + 1, g ^ other)
            elif c - 1 in lower:
                to = (c - 1, g ^ other)
            else:
                to = (c, g ^ 1 if g ^ 1 < group else g)
            pairs.append((c * group + g, to[0] * group + to[1]))
    return pairs


def one_way(lower, cuts, group):
    return [(lower * group + g, (lower + 1) * group + g) for g in range(group)]


def across(value, energy, group):
    points, members = lax.axis_size("energy"), lax.axis_size("group")
    pairs = [
        (e * members + g, (e + energy) % points * members + (g ^ group))
        for e in range(points)
        for g in range(members)
    ]
    return lax.ppermute(value, ("energy", "group"), pairs)


def body(transfer, source, coupling, strength, mode_shift):
    mats, srcs = transfer[0], source[0]
    width = srcs.shape[1]
    cuts, group, points = (lax.axis_size(a) for a in ("cuts", "group", "energy"))
    heights = heights_of(width)
    pieces = len(heights)
    middle, local, last, offsets = composites(mats, srcs, heights)
    leaving = first_chain(mats, srcs, heights[:1]) + offsets[1:]
    incoming, blocks = [None] * pieces, None
    for step in range(1, cuts):
        if step < cuts - 1:
            pairs = paired([step - 1], cuts, group)
        else:
            pairs = one_way(step - 1, cuts, group)
        got = [lax.ppermute(piece, ("cuts", "group"), pairs) for piece in leaving]
        if step < cuts - 1:
            leaving, after = [], last[0] if blocks is None else weights
            for piece in range(pieces):
                after, incoming[piece] = relay(
                    step, last, offsets[piece], got[piece], incoming[piece], after
                )
                leaving.append(after)
        if blocks is None:
            *blocks, weights = turned_blocks(
                mats, srcs, middle, local, strength[None], mode_shift[None], leaving[-1], points, 1.0 / (width * group)
            )
    green, sums = [], None
    for piece in range(pieces):
        part, sums = green_piece(
            cuts - 1, sum(heights[:piece]), blocks, last, offsets[piece], got[piece], incoming[piece], sums
        )
        green.append(part)

    other = 1 if group % 2 == 0 else 0
    if other:
        sums = sums + across(sums, 0, 1)
    sums = sums + sum(across(sums, 0, k + other) for k in range(1 + other, group, 1 + other))
    mixed = sums * weights[:1]
    for offset in range(1, points):
        mixed = mixed + across(sums, offset, other) * weights[offset : offset + 1]
    inner, kept = inner_blocks(coupling, green)
    edges = edge_rows(mixed, inner, cuts)
    after = [
        lax.ppermute(
            edges[lower], ("cuts", "group"), paired([lower], cuts, group, other)
        )
        for lower in range(cuts - 1)
    ]
    out, kept = early_blocks(coupling, inner, kept, mixed)
    scattered = late_blocks(coupling, inner, mixed, out, after)
    return kept[None], scattered[None]


def solution(mesh):
    in_specs = (P("energy", "cuts", None, None), P("energy", "cuts", "group"), P(), P(), P())
    out_specs = (P("energy", "cuts", "group"), P("energy", "cuts", "group"))
    return jax.shard_map(body, mesh=mesh, in_specs=in_specs, out_specs=out_specs, check_vma=False)
```

```python
import functools

import jax
import jax.numpy as jnp
from jax import lax
from jax.experimental import pallas as pl
from jax.experimental.pallas import tpu as pltpu
from jax.sharding import PartitionSpec as P

F32 = jnp.float32
BF16 = jnp.bfloat16
VMEM = pl.BlockSpec(memory_space=pltpu.VMEM)
HBM = pl.BlockSpec(memory_space=pltpu.HBM)
PARAMS = pltpu.CompilerParams(vmem_limit_bytes=32 * 1024 * 1024)
WHOLE = pltpu.CompilerParams(vmem_limit_bytes=107 * 512 * 1024)
SHARES = (9, 7)


def split(value):
    high = value.astype(BF16)
    return high, (value - high.astype(F32)).astype(BF16)


def dot(left, right):
    return jnp.dot(left, right, preferred_element_type=F32)


def dot_t(left, right):
    return lax.dot_general(left, right, (((1,), (1,)), ((), ())), preferred_element_type=F32)


def product(left_high, left_low, state):
    high, low = split(state)
    width = state.shape[1]
    both = dot(left_high, jnp.concatenate([high, low], axis=1))
    return both[:, :width] + (both[:, width:] + dot(left_low, high))


def product_rows(state, right_high, right_low):
    high, low = split(state)
    height = state.shape[0]
    both = dot(jnp.concatenate([high, low], axis=0), right_high)
    return both[:height] + (both[height:] + dot(high, right_low))


def chain_step(matrix, state, srcs):
    return product(*split(matrix), state) + srcs


def heights_of(width):
    if width % 8 or width // 8 < sum(SHARES):
        return (width,)
    ends = [8 * (width // 8 * sum(SHARES[: k + 1]) // sum(SHARES)) for k in range(len(SHARES))]
    return tuple(end - start for start, end in zip([0, *ends], ends))


def store_pieces(refs, state):
    turned = state.T
    start = 0
    for ref in refs:
        ref[...] = turned[start : start + ref.shape[0], :]
        start += ref.shape[0]


def first_kernel(mats_ref, srcs_ref, *rest):
    leaving_refs, (mats, srcs, sems, src_sem) = rest[:-4], rest[-4:]
    count, orbs = mats_ref.shape[0], mats_ref.shape[1]
    first = lax.axis_index("cuts") == 0

    @pl.when(first)
    def _():
        src_copy = pltpu.make_async_copy(srcs_ref, srcs, src_sem)
        copies = [
            pltpu.make_async_copy(mats_ref.at[k], mats.at[k], sems.at[k]) for k in range(1, count)
        ]
        src_copy.start()
        for copy in copies:
            copy.start()
        src_copy.wait()
        state = srcs[:orbs, :]
        for k in range(1, count):
            copies[k - 1].wait()
            state = chain_step(mats[k], state, srcs[k * orbs : (k + 1) * orbs, :])
        store_pieces(leaving_refs, state)

    @pl.when(jnp.logical_not(first))
    def _():
        for ref in leaving_refs:
            ref[...] = jnp.zeros_like(ref)


def first_chain(mats, srcs, heights):
    count, orbs, _ = mats.shape
    return list(
        pl.pallas_call(
            first_kernel,
            out_shape=tuple(jax.ShapeDtypeStruct((height, orbs), F32) for height in heights),
            in_specs=[HBM, HBM],
            out_specs=(VMEM,) * len(heights),
            scratch_shapes=[
                pltpu.VMEM(mats.shape, F32),
                pltpu.VMEM(srcs.shape, F32),
                pltpu.SemaphoreType.DMA((count,)),
                pltpu.SemaphoreType.DMA,
            ],
            compiler_params=WHOLE,
            name="first_chain",
        )(mats, srcs)
    )


def composite_kernel(mats_ref, srcs_ref, middle_ref, local_ref, high_ref, low_ref, *offset_refs):
    full = mats_ref[0]
    count, orbs = mats_ref.shape[0], mats_ref.shape[1]
    state = srcs_ref[:orbs, :]
    for k in range(1, count):
        left_high, left_low = split(mats_ref[k])
        state = product(left_high, left_low, state) + srcs_ref[k * orbs : (k + 1) * orbs, :]
        high, low = split(full)
        full = dot(left_high, high) + (dot(left_high, low) + dot(left_low, high))
        if k < count - 1:
            middle_ref[k - 1] = full
            local_ref[k - 1] = state
    store_pieces(offset_refs, state)
    high_ref[...], low_ref[...] = split(full.T)


def composites(mats, srcs, heights):
    count, orbs, _ = mats.shape
    width = srcs.shape[1]
    shape = jax.ShapeDtypeStruct((orbs, orbs), BF16)
    outs = pl.pallas_call(
        composite_kernel,
        out_shape=(
            jax.ShapeDtypeStruct((count - 2, orbs, orbs), F32),
            jax.ShapeDtypeStruct((count - 2, orbs, width), F32),
            shape,
            shape,
        )
        + tuple(jax.ShapeDtypeStruct((height, orbs), F32) for height in heights),
        in_specs=[VMEM, VMEM],
        out_specs=(VMEM,) * (4 + len(heights)),
        compiler_params=PARAMS,
        cost_estimate=pl.CostEstimate(
            flops=6 * (count - 1) * orbs**3, bytes_accessed=8 * count * orbs**2, transcendentals=0
        ),
        name="composites",
    )(mats, srcs)
    return outs[0], outs[1], outs[2:4], list(outs[4:])


def turned_kernel(
    points, scale, first_ref, srcs_ref, mats_ref, local_ref, strength_ref, shift_ref, _, high_ref, low_ref, turned_ref, weight_ref
):
    orbs = first_ref.shape[1]
    here = lax.axis_index("energy")
    goal = here + shift_ref[...]
    goal = jnp.where(goal >= points, goal - points, goal)
    for offset in range(points):
        from_here = lax.rem(here + points - offset, points)
        total = jnp.sum(
            jnp.where(goal == from_here, strength_ref[...], 0.0), axis=1, keepdims=True
        )
        weight_ref[offset : offset + 1, :] = jnp.broadcast_to(total * scale, (1, orbs))
    for k in range(mats_ref.shape[0] + 1):
        columns = slice(k * orbs, (k + 1) * orbs)
        matrix = first_ref[0] if k == 0 else mats_ref[k - 1]
        local = srcs_ref[:orbs, :] if k == 0 else local_ref[k - 1]
        high_ref[:, columns], low_ref[:, columns] = split(matrix.T)
        turned_ref[:, columns] = local.T


def turned_blocks(mats, srcs, middle, local, strength, shift, after, points, scale):
    count, orbs, _ = mats.shape
    width = srcs.shape[1]
    length = (count - 1) * orbs
    shape = jax.ShapeDtypeStruct((orbs, length), BF16)
    return pl.pallas_call(
        functools.partial(turned_kernel, points, scale),
        out_shape=(
            shape,
            shape,
            jax.ShapeDtypeStruct((width, length), F32),
            jax.ShapeDtypeStruct((points, orbs), F32),
        ),
        in_specs=[VMEM] * 7,
        out_specs=(VMEM,) * 4,
        compiler_params=PARAMS,
        name="turned_blocks",
    )(mats, srcs, middle, local, strength, shift, after)


def relay_kernel(step, first, high_ref, low_ref, offset_ref, got_ref, _, *rest):
    out_ref, kept_ref = rest[-2:]
    got = got_ref[...]
    out_ref[...] = product_rows(got, high_ref[...], low_ref[...]) + offset_ref[...]
    other = 0.0 if first else rest[0][...]
    kept_ref[...] = jnp.where(lax.axis_index("cuts") == step, got, other)


def relay(step, last, offset, got, incoming, after):
    shape = jax.ShapeDtypeStruct(got.shape, F32)
    args = [*last, offset, got, after] + ([] if incoming is None else [incoming])
    return pl.pallas_call(
        functools.partial(relay_kernel, step, incoming is None),
        out_shape=(shape, shape),
        in_specs=[VMEM] * len(args),
        out_specs=(VMEM, VMEM),
        compiler_params=PARAMS,
        name="relay",
    )(*args)


def green_kernel(
    step, start, high_ref, low_ref, turned_ref, last_high_ref, last_low_ref, offset_ref, got_ref, incoming_ref, *rest
):
    green_ref, sums_ref = rest[-2:]
    height, orbs = got_ref.shape
    length = high_ref.shape[1]
    rows = slice(start, start + height)
    state = jnp.where(lax.axis_index("cuts") == step, got_ref[...], incoming_ref[...])
    sums = [jnp.sum(state * state, axis=0, keepdims=True)]
    green = product_rows(state, high_ref[...], low_ref[...]) + turned_ref[rows, :]
    green_ref[:, :length] = green
    for k in range(length // orbs):
        block = green[:, k * orbs : (k + 1) * orbs]
        sums.append(jnp.sum(block * block, axis=0, keepdims=True))
    block = product_rows(state, last_high_ref[...], last_low_ref[...]) + offset_ref[...]
    green_ref[:, length:] = block
    sums.append(jnp.sum(block * block, axis=0, keepdims=True))
    total = jnp.concatenate(sums, axis=0)
    sums_ref[...] = total if len(rest) == 2 else total + rest[0][...]


def green_piece(step, start, blocks, last, offset, got, incoming, sums):
    height, orbs = got.shape
    count = blocks[0].shape[1] // orbs + 1
    args = [*blocks, *last, offset, got, incoming] + ([] if sums is None else [sums])
    return pl.pallas_call(
        functools.partial(green_kernel, step, start),
        out_shape=(
            jax.ShapeDtypeStruct((height, count * orbs), F32),
            jax.ShapeDtypeStruct((count + 1, orbs), F32),
        ),
        in_specs=[VMEM] * len(args),
        out_specs=(VMEM, VMEM),
        compiler_params=PARAMS,
        name="green_piece",
    )(*args)


def inner_kernel(coupling_ref, *rest):
    green_refs, (inner_ref, turned_ref) = rest[:-2], rest[-2:]
    orbs = coupling_ref.shape[0]
    coupling = coupling_ref[...]
    green = jnp.concatenate([g[...] for g in green_refs], axis=0)
    low = green.astype(BF16)
    for k in range(low.shape[1] // orbs):
        columns = slice(k * orbs, (k + 1) * orbs)
        inner_ref[:, columns] = dot(low[:, columns], coupling)
        turned_ref[columns, :] = green[:, columns].T


def inner_blocks(coupling, pieces):
    length = pieces[0].shape[1]
    width = sum(piece.shape[0] for piece in pieces)
    return pl.pallas_call(
        inner_kernel,
        out_shape=(
            jax.ShapeDtypeStruct((width, length), F32),
            jax.ShapeDtypeStruct((length, width), F32),
        ),
        in_specs=[VMEM] * (1 + len(pieces)),
        out_specs=(VMEM, VMEM),
        compiler_params=PARAMS,
        cost_estimate=pl.CostEstimate(
            flops=2 * width * length * coupling.shape[0], bytes_accessed=12 * width * length, transcendentals=0
        ),
        name="inner_blocks",
    )(coupling, *pieces)


def smoothed(rows, k):
    return rows[k + 1] + 0.5 * (rows[k] + rows[k + 2])


def scattered_block(coupling, inner_ref, rows, k):
    orbs = coupling.shape[0]
    columns = slice(k * orbs, (k + 1) * orbs)
    return dot_t(coupling, (inner_ref[:, columns] * smoothed(rows, k)).astype(BF16))


def early_kernel(coupling_ref, inner_ref, green_ref, mixed_ref, out_ref, kept_ref, staged, sems, kept_sem):
    kept_copy = pltpu.make_async_copy(green_ref, kept_ref, kept_sem)
    kept_copy.start()
    orbs = coupling_ref.shape[0]
    count = inner_ref.shape[1] // orbs
    coupling = coupling_ref[...]
    rows = [mixed_ref[k : k + 1, :] for k in range(count + 1)]
    rows.append(jnp.zeros_like(rows[0]))
    last = lax.axis_index("cuts") == lax.axis_size("cuts") - 1

    def block_copy(k):
        columns = slice(k * orbs, (k + 1) * orbs)
        return pltpu.make_async_copy(staged.at[columns], out_ref.at[columns], sems.at[k])

    def block_start(k):
        staged[k * orbs : (k + 1) * orbs, :] = scattered_block(coupling, inner_ref, rows, k)
        block_copy(k).start()

    for k in range(count - 1):
        block_start(k)

    @pl.when(last)
    def _():
        block_start(count - 1)

    for k in range(count - 1):
        block_copy(k).wait()

    @pl.when(last)
    def _():
        block_copy(count - 1).wait()

    kept_copy.wait()


def early_blocks(coupling, inner, green, mixed):
    width, length = inner.shape
    orbs = coupling.shape[0]
    shape = jax.ShapeDtypeStruct((length, width), F32)
    return pl.pallas_call(
        early_kernel,
        out_shape=(shape, shape),
        in_specs=[VMEM] * 4,
        out_specs=(HBM, HBM),
        scratch_shapes=[
            pltpu.VMEM((length, width), F32),
            pltpu.SemaphoreType.DMA((length // orbs,)),
            pltpu.SemaphoreType.DMA,
        ],
        compiler_params=PARAMS,
        name="early_blocks",
    )(coupling, inner, green, mixed)


def late_kernel(coupling_ref, inner_ref, mixed_ref, _, *rest):
    *after_refs, out_ref, block, sem = rest
    orbs = coupling_ref.shape[0]
    count = inner_ref.shape[1] // orbs
    here = lax.axis_index("cuts")

    @pl.when(here < lax.axis_size("cuts") - 1)
    def _():
        after = jnp.zeros((1, orbs), F32)
        for lower, after_ref in enumerate(after_refs):
            after = jnp.where(here == lower, after_ref[:1, :], after)
        rows = [mixed_ref[k : k + 1, :] for k in range(count + 1)] + [after]
        block[...] = scattered_block(coupling_ref[...], inner_ref, rows, count - 1)
        copy = pltpu.make_async_copy(block, out_ref.at[slice((count - 1) * orbs, count * orbs)], sem)
        copy.start()
        copy.wait()


def late_blocks(coupling, inner, mixed, out, after):
    orbs = coupling.shape[0]
    return pl.pallas_call(
        late_kernel,
        out_shape=jax.ShapeDtypeStruct(out.shape, F32),
        in_specs=[VMEM] * 3 + [HBM] + [VMEM] * len(after),
        out_specs=HBM,
        scratch_shapes=[pltpu.VMEM((orbs, out.shape[1]), F32), pltpu.SemaphoreType.DMA],
        input_output_aliases={3: 0},
        compiler_params=PARAMS,
        name="late_blocks",
    )(coupling, inner, mixed, out, *after)


def edge_kernel(mixed_ref, _, *out_refs):
    for out_ref in out_refs:
        out_ref[...] = jnp.broadcast_to(mixed_ref[1:2, :], out_ref.shape)


def edge_rows(mixed, after, cuts):
    return pl.pallas_call(
        edge_kernel,
        out_shape=tuple(
            jax.ShapeDtypeStruct((4 * (cuts - 1 - lower), mixed.shape[1]), F32)
            for lower in range(cuts - 1)
        ),
        in_specs=[VMEM, VMEM],
        out_specs=(VMEM,) * (cuts - 1),
        compiler_params=PARAMS,
        name="edge_rows",
    )(mixed, after)


def paired(lower, cuts, group, other=0):
    pairs = []
    for c in range(cuts):
        for g in range(group):
            if c in lower:
                to = (c + 1, g ^ other)
            elif c - 1 in lower:
                to = (c - 1, g ^ other)
            else:
                to = (c, g ^ 1 if g ^ 1 < group else g)
            pairs.append((c * group + g, to[0] * group + to[1]))
    return pairs


def one_way(lower, cuts, group):
    return [(lower * group + g, (lower + 1) * group + g) for g in range(group)]


def across(value, energy, group):
    points, members = lax.axis_size("energy"), lax.axis_size("group")
    pairs = [
        (e * members + g, (e + energy) % points * members + (g ^ group))
        for e in range(points)
        for g in range(members)
    ]
    return lax.ppermute(value, ("energy", "group"), pairs)


def body(transfer, source, coupling, strength, mode_shift):
    mats, srcs = transfer[0], source[0]
    width = srcs.shape[1]
    cuts, group, points = (lax.axis_size(a) for a in ("cuts", "group", "energy"))
    heights = heights_of(width)
    pieces = len(heights)
    middle, local, last, offsets = composites(mats, srcs, heights)
    leaving = first_chain(mats, srcs, heights[:1]) + offsets[1:]
    incoming, blocks = [None] * pieces, None
    for step in range(1, cuts):
        if step < cuts - 1:
            pairs = paired([step - 1], cuts, group)
        else:
            pairs = one_way(step - 1, cuts, group)
        got = [lax.ppermute(piece, ("cuts", "group"), pairs) for piece in leaving]
        if step < cuts - 1:
            leaving, after = [], last[0] if blocks is None else weights
            for piece in range(pieces):
                after, incoming[piece] = relay(
                    step, last, offsets[piece], got[piece], incoming[piece], after
                )
                leaving.append(after)
        if blocks is None:
            *blocks, weights = turned_blocks(
                mats, srcs, middle, local, strength[None], mode_shift[None], leaving[-1], points, 1.0 / (width * group)
            )
    green, sums = [], None
    for piece in range(pieces):
        part, sums = green_piece(
            cuts - 1, sum(heights[:piece]), blocks, last, offsets[piece], got[piece], incoming[piece], sums
        )
        green.append(part)

    other = 1 if group % 2 == 0 else 0
    sums = sums + sum(across(sums, 0, k + other) for k in range(1 + other, group, 1 + other))
    mixed = sums * weights[:1]
    for offset in range(1, points):
        mixed = mixed + across(sums, offset, other) * weights[offset : offset + 1]
    if other:
        mixed = mixed + across(mixed, 0, 1)
    inner, kept = inner_blocks(coupling, green)
    edges = edge_rows(mixed, inner, cuts)
    after = [
        lax.ppermute(
            edges[lower], ("cuts", "group"), paired([lower], cuts, group, other)
        )
        for lower in range(cuts - 1)
    ]
    out, kept = early_blocks(coupling, inner, kept, mixed)
    scattered = late_blocks(coupling, inner, mixed, out, after)
    return kept[None], scattered[None]


def solution(mesh):
    in_specs = (P("energy", "cuts", None, None), P("energy", "cuts", "group"), P(), P(), P())
    out_specs = (P("energy", "cuts", "group"), P("energy", "cuts", "group"))
    return jax.shard_map(body, mesh=mesh, in_specs=in_specs, out_specs=out_specs, check_vma=False)
```

```python
import functools

import jax
import jax.numpy as jnp
from jax import lax
from jax.experimental import pallas as pl
from jax.experimental.pallas import tpu as pltpu
from jax.sharding import PartitionSpec as P

F32 = jnp.float32
BF16 = jnp.bfloat16
VMEM = pl.BlockSpec(memory_space=pltpu.VMEM)
HBM = pl.BlockSpec(memory_space=pltpu.HBM)
PARAMS = pltpu.CompilerParams(vmem_limit_bytes=32 * 1024 * 1024)
WHOLE = pltpu.CompilerParams(vmem_limit_bytes=107 * 512 * 1024)
SHARES = (1, 1)


def split(value):
    high = value.astype(BF16)
    return high, (value - high.astype(F32)).astype(BF16)


def dot(left, right):
    return jnp.dot(left, right, preferred_element_type=F32)


def dot_t(left, right):
    return lax.dot_general(left, right, (((1,), (1,)), ((), ())), preferred_element_type=F32)


def product(left_high, left_low, state):
    high, low = split(state)
    width = state.shape[1]
    both = dot(left_high, jnp.concatenate([high, low], axis=1))
    return both[:, :width] + (both[:, width:] + dot(left_low, high))


def product_rows(state, right_high, right_low):
    high, low = split(state)
    height = state.shape[0]
    both = dot(jnp.concatenate([high, low], axis=0), right_high)
    return both[:height] + (both[height:] + dot(high, right_low))


def chain_step(matrix, state, srcs):
    return product(*split(matrix), state) + srcs


def heights_of(width):
    if width % 8 or width // 8 < sum(SHARES):
        return (width,)
    ends = [8 * (width // 8 * sum(SHARES[: k + 1]) // sum(SHARES)) for k in range(len(SHARES))]
    return tuple(end - start for start, end in zip([0, *ends], ends))


def store_pieces(refs, state):
    turned = state.T
    start = 0
    for ref in refs:
        ref[...] = turned[start : start + ref.shape[0], :]
        start += ref.shape[0]


def first_kernel(mats_ref, srcs_ref, *rest):
    leaving_refs, (mats, srcs, sems, src_sem) = rest[:-4], rest[-4:]
    count, orbs = mats_ref.shape[0], mats_ref.shape[1]
    first = lax.axis_index("cuts") == 0

    @pl.when(first)
    def _():
        src_copy = pltpu.make_async_copy(srcs_ref, srcs, src_sem)
        copies = [
            pltpu.make_async_copy(mats_ref.at[k], mats.at[k], sems.at[k]) for k in range(1, count)
        ]
        src_copy.start()
        for copy in copies:
            copy.start()
        src_copy.wait()
        state = srcs[:orbs, :]
        for k in range(1, count):
            copies[k - 1].wait()
            state = chain_step(mats[k], state, srcs[k * orbs : (k + 1) * orbs, :])
        store_pieces(leaving_refs, state)

    @pl.when(jnp.logical_not(first))
    def _():
        for ref in leaving_refs:
            ref[...] = jnp.zeros_like(ref)


def first_chain(mats, srcs, heights):
    count, orbs, _ = mats.shape
    return list(
        pl.pallas_call(
            first_kernel,
            out_shape=tuple(jax.ShapeDtypeStruct((height, orbs), F32) for height in heights),
            in_specs=[HBM, HBM],
            out_specs=(VMEM,) * len(heights),
            scratch_shapes=[
                pltpu.VMEM(mats.shape, F32),
                pltpu.VMEM(srcs.shape, F32),
                pltpu.SemaphoreType.DMA((count,)),
                pltpu.SemaphoreType.DMA,
            ],
            compiler_params=WHOLE,
            name="first_chain",
        )(mats, srcs)
    )


def composite_kernel(mats_ref, srcs_ref, middle_ref, local_ref, high_ref, low_ref, *offset_refs):
    full = mats_ref[0]
    count, orbs = mats_ref.shape[0], mats_ref.shape[1]
    state = srcs_ref[:orbs, :]
    for k in range(1, count):
        left_high, left_low = split(mats_ref[k])
        state = product(left_high, left_low, state) + srcs_ref[k * orbs : (k + 1) * orbs, :]
        high, low = split(full)
        full = dot(left_high, high) + (dot(left_high, low) + dot(left_low, high))
        if k < count - 1:
            middle_ref[k - 1] = full
            local_ref[k - 1] = state
    store_pieces(offset_refs, state)
    high_ref[...], low_ref[...] = split(full.T)


def composites(mats, srcs, heights):
    count, orbs, _ = mats.shape
    width = srcs.shape[1]
    shape = jax.ShapeDtypeStruct((orbs, orbs), BF16)
    outs = pl.pallas_call(
        composite_kernel,
        out_shape=(
            jax.ShapeDtypeStruct((count - 2, orbs, orbs), F32),
            jax.ShapeDtypeStruct((count - 2, orbs, width), F32),
            shape,
            shape,
        )
        + tuple(jax.ShapeDtypeStruct((height, orbs), F32) for height in heights),
        in_specs=[VMEM, VMEM],
        out_specs=(VMEM,) * (4 + len(heights)),
        compiler_params=PARAMS,
        cost_estimate=pl.CostEstimate(
            flops=6 * (count - 1) * orbs**3, bytes_accessed=8 * count * orbs**2, transcendentals=0
        ),
        name="composites",
    )(mats, srcs)
    return outs[0], outs[1], outs[2:4], list(outs[4:])


def turned_kernel(
    points, scale, first_ref, srcs_ref, mats_ref, local_ref, strength_ref, shift_ref, _, high_ref, low_ref, turned_ref, weight_ref
):
    orbs = first_ref.shape[1]
    here = lax.axis_index("energy")
    goal = here + shift_ref[...]
    goal = jnp.where(goal >= points, goal - points, goal)
    for offset in range(points):
        from_here = lax.rem(here + points - offset, points)
        total = jnp.sum(
            jnp.where(goal == from_here, strength_ref[...], 0.0), axis=1, keepdims=True
        )
        weight_ref[offset : offset + 1, :] = jnp.broadcast_to(total * scale, (1, orbs))
    for k in range(mats_ref.shape[0] + 1):
        columns = slice(k * orbs, (k + 1) * orbs)
        matrix = first_ref[0] if k == 0 else mats_ref[k - 1]
        local = srcs_ref[:orbs, :] if k == 0 else local_ref[k - 1]
        high_ref[:, columns], low_ref[:, columns] = split(matrix.T)
        turned_ref[:, columns] = local.T


def turned_blocks(mats, srcs, middle, local, strength, shift, after, points, scale):
    count, orbs, _ = mats.shape
    width = srcs.shape[1]
    length = (count - 1) * orbs
    shape = jax.ShapeDtypeStruct((orbs, length), BF16)
    return pl.pallas_call(
        functools.partial(turned_kernel, points, scale),
        out_shape=(
            shape,
            shape,
            jax.ShapeDtypeStruct((width, length), F32),
            jax.ShapeDtypeStruct((points, orbs), F32),
        ),
        in_specs=[VMEM] * 7,
        out_specs=(VMEM,) * 4,
        compiler_params=PARAMS,
        name="turned_blocks",
    )(mats, srcs, middle, local, strength, shift, after)


def relay_kernel(step, first, high_ref, low_ref, offset_ref, got_ref, _, *rest):
    out_ref, kept_ref = rest[-2:]
    got = got_ref[...]
    out_ref[...] = product_rows(got, high_ref[...], low_ref[...]) + offset_ref[...]
    other = 0.0 if first else rest[0][...]
    kept_ref[...] = jnp.where(lax.axis_index("cuts") == step, got, other)


def relay(step, last, offset, got, incoming, after):
    shape = jax.ShapeDtypeStruct(got.shape, F32)
    args = [*last, offset, got, after] + ([] if incoming is None else [incoming])
    return pl.pallas_call(
        functools.partial(relay_kernel, step, incoming is None),
        out_shape=(shape, shape),
        in_specs=[VMEM] * len(args),
        out_specs=(VMEM, VMEM),
        compiler_params=PARAMS,
        name="relay",
    )(*args)


def green_kernel(
    step, start, high_ref, low_ref, turned_ref, last_high_ref, last_low_ref, offset_ref, got_ref, incoming_ref, *rest
):
    green_ref, sums_ref = rest[-2:]
    height, orbs = got_ref.shape
    length = high_ref.shape[1]
    rows = slice(start, start + height)
    state = jnp.where(lax.axis_index("cuts") == step, got_ref[...], incoming_ref[...])
    sums = [jnp.sum(state * state, axis=0, keepdims=True)]
    green = product_rows(state, high_ref[...], low_ref[...]) + turned_ref[rows, :]
    green_ref[:, :length] = green
    for k in range(length // orbs):
        block = green[:, k * orbs : (k + 1) * orbs]
        sums.append(jnp.sum(block * block, axis=0, keepdims=True))
    block = product_rows(state, last_high_ref[...], last_low_ref[...]) + offset_ref[...]
    green_ref[:, length:] = block
    sums.append(jnp.sum(block * block, axis=0, keepdims=True))
    total = jnp.concatenate(sums, axis=0)
    sums_ref[...] = total if len(rest) == 2 else total + rest[0][...]


def green_piece(step, start, blocks, last, offset, got, incoming, sums):
    height, orbs = got.shape
    count = blocks[0].shape[1] // orbs + 1
    args = [*blocks, *last, offset, got, incoming] + ([] if sums is None else [sums])
    return pl.pallas_call(
        functools.partial(green_kernel, step, start),
        out_shape=(
            jax.ShapeDtypeStruct((height, count * orbs), F32),
            jax.ShapeDtypeStruct((count + 1, orbs), F32),
        ),
        in_specs=[VMEM] * len(args),
        out_specs=(VMEM, VMEM),
        compiler_params=PARAMS,
        name="green_piece",
    )(*args)


def inner_kernel(coupling_ref, *rest):
    green_refs, (inner_ref, turned_ref) = rest[:-2], rest[-2:]
    orbs = coupling_ref.shape[0]
    coupling = coupling_ref[...]
    green = jnp.concatenate([g[...] for g in green_refs], axis=0)
    low = green.astype(BF16)
    for k in range(low.shape[1] // orbs):
        columns = slice(k * orbs, (k + 1) * orbs)
        inner_ref[:, columns] = dot(low[:, columns], coupling)
        turned_ref[columns, :] = green[:, columns].T


def inner_blocks(coupling, pieces):
    length = pieces[0].shape[1]
    width = sum(piece.shape[0] for piece in pieces)
    return pl.pallas_call(
        inner_kernel,
        out_shape=(
            jax.ShapeDtypeStruct((width, length), F32),
            jax.ShapeDtypeStruct((length, width), F32),
        ),
        in_specs=[VMEM] * (1 + len(pieces)),
        out_specs=(VMEM, VMEM),
        compiler_params=PARAMS,
        cost_estimate=pl.CostEstimate(
            flops=2 * width * length * coupling.shape[0], bytes_accessed=12 * width * length, transcendentals=0
        ),
        name="inner_blocks",
    )(coupling, *pieces)


def smoothed(rows, k):
    return rows[k + 1] + 0.5 * (rows[k] + rows[k + 2])


def scattered_block(coupling, inner_ref, rows, k):
    orbs = coupling.shape[0]
    columns = slice(k * orbs, (k + 1) * orbs)
    return dot_t(coupling, (inner_ref[:, columns] * smoothed(rows, k)).astype(BF16))


def early_kernel(coupling_ref, inner_ref, green_ref, mixed_ref, out_ref, kept_ref, staged, sems, kept_sem):
    kept_copy = pltpu.make_async_copy(green_ref, kept_ref, kept_sem)
    kept_copy.start()
    orbs = coupling_ref.shape[0]
    count = inner_ref.shape[1] // orbs
    coupling = coupling_ref[...]
    rows = [mixed_ref[k : k + 1, :] for k in range(count + 1)]
    rows.append(jnp.zeros_like(rows[0]))
    last = lax.axis_index("cuts") == lax.axis_size("cuts") - 1

    def block_copy(k):
        columns = slice(k * orbs, (k + 1) * orbs)
        return pltpu.make_async_copy(staged.at[columns], out_ref.at[columns], sems.at[k])

    def block_start(k):
        staged[k * orbs : (k + 1) * orbs, :] = scattered_block(coupling, inner_ref, rows, k)
        block_copy(k).start()

    for k in range(count - 1):
        block_start(k)

    @pl.when(last)
    def _():
        block_start(count - 1)

    for k in range(count - 1):
        block_copy(k).wait()

    @pl.when(last)
    def _():
        block_copy(count - 1).wait()

    kept_copy.wait()


def early_blocks(coupling, inner, green, mixed):
    width, length = inner.shape
    orbs = coupling.shape[0]
    shape = jax.ShapeDtypeStruct((length, width), F32)
    return pl.pallas_call(
        early_kernel,
        out_shape=(shape, shape),
        in_specs=[VMEM] * 4,
        out_specs=(HBM, HBM),
        scratch_shapes=[
            pltpu.VMEM((length, width), F32),
            pltpu.SemaphoreType.DMA((length // orbs,)),
            pltpu.SemaphoreType.DMA,
        ],
        compiler_params=PARAMS,
        name="early_blocks",
    )(coupling, inner, green, mixed)


def late_kernel(coupling_ref, inner_ref, mixed_ref, _, *rest):
    *after_refs, out_ref, block, sem = rest
    orbs = coupling_ref.shape[0]
    count = inner_ref.shape[1] // orbs
    here = lax.axis_index("cuts")

    @pl.when(here < lax.axis_size("cuts") - 1)
    def _():
        after = jnp.zeros((1, orbs), F32)
        for lower, after_ref in enumerate(after_refs):
            after = jnp.where(here == lower, after_ref[:1, :], after)
        rows = [mixed_ref[k : k + 1, :] for k in range(count + 1)] + [after]
        block[...] = scattered_block(coupling_ref[...], inner_ref, rows, count - 1)
        copy = pltpu.make_async_copy(block, out_ref.at[slice((count - 1) * orbs, count * orbs)], sem)
        copy.start()
        copy.wait()


def late_blocks(coupling, inner, mixed, out, after):
    orbs = coupling.shape[0]
    return pl.pallas_call(
        late_kernel,
        out_shape=jax.ShapeDtypeStruct(out.shape, F32),
        in_specs=[VMEM] * 3 + [HBM] + [VMEM] * len(after),
        out_specs=HBM,
        scratch_shapes=[pltpu.VMEM((orbs, out.shape[1]), F32), pltpu.SemaphoreType.DMA],
        input_output_aliases={3: 0},
        compiler_params=PARAMS,
        name="late_blocks",
    )(coupling, inner, mixed, out, *after)


def edge_kernel(mixed_ref, _, *out_refs):
    for out_ref in out_refs:
        out_ref[...] = jnp.broadcast_to(mixed_ref[1:2, :], out_ref.shape)


def edge_rows(mixed, after, cuts):
    return pl.pallas_call(
        edge_kernel,
        out_shape=tuple(
            jax.ShapeDtypeStruct((4 * (cuts - 1 - lower), mixed.shape[1]), F32)
            for lower in range(cuts - 1)
        ),
        in_specs=[VMEM, VMEM],
        out_specs=(VMEM,) * (cuts - 1),
        compiler_params=PARAMS,
        name="edge_rows",
    )(mixed, after)


def paired(lower, cuts, group, other=0):
    pairs = []
    for c in range(cuts):
        for g in range(group):
            if c in lower:
                to = (c + 1, g ^ other)
            elif c - 1 in lower:
                to = (c - 1, g ^ other)
            else:
                to = (c, g ^ 1 if g ^ 1 < group else g)
            pairs.append((c * group + g, to[0] * group + to[1]))
    return pairs


def one_way(lower, cuts, group):
    return [(lower * group + g, (lower + 1) * group + g) for g in range(group)]


def across(value, energy, group):
    points, members = lax.axis_size("energy"), lax.axis_size("group")
    pairs = [
        (e * members + g, (e + energy) % points * members + (g ^ group))
        for e in range(points)
        for g in range(members)
    ]
    return lax.ppermute(value, ("energy", "group"), pairs)


def body(transfer, source, coupling, strength, mode_shift):
    mats, srcs = transfer[0], source[0]
    width = srcs.shape[1]
    cuts, group, points = (lax.axis_size(a) for a in ("cuts", "group", "energy"))
    heights = heights_of(width)
    pieces = len(heights)
    middle, local, last, offsets = composites(mats, srcs, heights)
    leaving = first_chain(mats, srcs, heights[:1]) + offsets[1:]
    incoming, blocks = [None] * pieces, None
    for step in range(1, cuts):
        if step < cuts - 1:
            pairs = paired([step - 1], cuts, group)
        else:
            pairs = one_way(step - 1, cuts, group)
        got = [lax.ppermute(piece, ("cuts", "group"), pairs) for piece in leaving]
        if step < cuts - 1:
            leaving, after = [], last[0] if blocks is None else weights
            for piece in range(pieces):
                after, incoming[piece] = relay(
                    step, last, offsets[piece], got[piece], incoming[piece], after
                )
                leaving.append(after)
        if blocks is None:
            *blocks, weights = turned_blocks(
                mats, srcs, middle, local, strength[None], mode_shift[None], leaving[-1], points, 1.0 / (width * group)
            )
    green, sums = [], None
    for piece in range(pieces):
        part, sums = green_piece(
            cuts - 1, sum(heights[:piece]), blocks, last, offsets[piece], got[piece], incoming[piece], sums
        )
        green.append(part)

    other = 1 if group % 2 == 0 else 0
    sums = sums + sum(across(sums, 0, k + other) for k in range(1 + other, group, 1 + other))
    mixed = sums * weights[:1]
    for offset in range(1, points):
        mixed = mixed + across(sums, offset, other) * weights[offset : offset + 1]
    if other:
        mixed = mixed + across(mixed, 0, 1)
    inner, kept = inner_blocks(coupling, green)
    edges = edge_rows(mixed, inner, cuts)
    after = [
        lax.ppermute(
            edges[lower], ("cuts", "group"), paired([lower], cuts, group, other)
        )
        for lower in range(cuts - 1)
    ]
    out, kept = early_blocks(coupling, inner, kept, mixed)
    scattered = late_blocks(coupling, inner, mixed, out, after)
    return kept[None], scattered[None]


def solution(mesh):
    in_specs = (P("energy", "cuts", None, None), P("energy", "cuts", "group"), P(), P(), P())
    out_specs = (P("energy", "cuts", "group"), P("energy", "cuts", "group"))
    return jax.shard_map(body, mesh=mesh, in_specs=in_specs, out_specs=out_specs, check_vma=False)
```
